512 devices in a mesh: ctx: 64 (over z, x), tp: 8 (over y, core).
Axes of the slice: x: 4, y: 4, z: 16, core: 2. Of those that a mesh axis runs over, the one named last changes fastest.
Arguments:
- new_hidden: bfloat16 [3, 4, 8192], P(None, None, 'ctx'), may hold values from -40 to 40
- norm_gain: float32 [8192], P('ctx'), may hold values from 0.5 to 1.5
- qkv_weight: bfloat16 [8192, 8, 1280], P('ctx', 'tp'), may hold values from -0.0625 to 0.0625
- out_weight: bfloat16 [8, 1024, 8192], P('tp', None, 'ctx'), may hold values from -0.0625 to 0.0625
- owned_cache: bfloat16 [8192, 16, 8, 256], P('ctx', None, 'tp'), may hold values from -128 to 128, as said below
- lengths: int32 [4], replicated, may hold values from 1 to 32768, as said below
- owner_device: int32 [64], replicated, may hold values from 0 to 63, each once
- block_target: int32 [8192, 1], replicated, may hold values from 0 to 63; in each aligned block of 128 rows (0 to 127, 128 to 255, ...) at most 2 rows name the same one
Outputs:
- attended: bfloat16 [3, 4, 8192], P(None, None, 'ctx')
- relaid_cache: bfloat16 [8192, 16, 8, 256], P('ctx', None, 'tp')
The draws below stay inside these ranges and needn't reach their ends.
Inputs may be any that keep to these rules, and one draw needn't show every extreme that they name: `owned_cache`: keys fill the first 128 entries of the last dimension, values the rest; entries past a sequence's length are not read. `lengths`: one sequence has exactly 32768 cached tokens; another has at most 8. `owner_device`: each device holds exactly one segment. `block_target`: among the 128 rows of each device every device number stands exactly 2 times.
All inputs are finite; a program needn't handle non-finite values.
Results may differ from the reference program's by a relative error of at most 0.01705.
The reference program's roundings to bfloat16 on the way (of `scaled`, `queries` and `attention`) count: a program that leaves them out, or rounds other values in their place, can miss the bound.
Values may be sent and summed in bfloat16 or wider, within the bound.
A program may use at most 64 MiB of HBM per device.

```python
import math
import jax
import jax.numpy as jnp
import numpy as np
from jax import lax

D = 8192
H = 64
KVH = 8
HD = 128
SEGLEN = 2048
SEQS = 4
STEPS = 3
CAP = 2
GROUP = 8
SEGS = 16
MAXLEN = 32768
OWN_BLK = 128
BLOCK = 16
N_CTX = 64


def draw_new_hidden(key, part):
    key = jax.random.fold_in(key, 11)
    key_basic, key_rough = jax.random.split(key, 2)
    column = jnp.arange(D, dtype=jnp.float32) / D
    roughness = jax.random.uniform(key_rough, (D,), jnp.float32, 0.6, 1.4)
    basic_draw = jax.random.truncated_normal(key_basic, -6.0, 6.0, (STEPS, SEQS, D), jnp.float32)
    values = basic_draw * jnp.sqrt(1.0 + 2.0 * column) * roughness
    return values.astype(jnp.bfloat16)


def draw_owned_cache(key, part):
    key = jax.random.fold_in(key, 23)
    key_keys, key_values = jax.random.split(key, 2)
    shape = (N_CTX * OWN_BLK, BLOCK, KVH, HD)
    keys_part = 2.0 * jax.random.truncated_normal(key_keys, -6.0, 6.0, shape, jnp.float32)
    values_part = jax.random.truncated_normal(key_values, -6.0, 6.0, shape, jnp.float32)
    return jnp.concatenate([keys_part, values_part], axis=-1).astype(jnp.bfloat16)


def draw_lengths(key, part):
    key = jax.random.fold_in(key, 37)
    first_key, second_key, pick_key, other_key, short_key = jax.random.split(key, 5)
    first = jax.random.randint(first_key, (SEQS,), 1, MAXLEN + 1)
    second = jax.random.randint(second_key, (SEQS,), 1, MAXLEN + 1)
    result = (first + jnp.minimum(first, second)) // 2
    chosen = jax.random.randint(pick_key, (), 0, SEQS)
    shifted = jax.random.randint(other_key, (), 1, SEQS)
    short_index = (chosen + shifted) % SEQS
    short_length = jax.random.randint(short_key, (), 1, 9)
    positions = jnp.arange(SEQS)
    result = jnp.where(positions == short_index, short_length, result)
    result = jnp.where(positions == chosen, MAXLEN, result)
    return result.astype(jnp.int32)


def steps_of(key, shape, pieces, low, top_value):
    loudness, own = 1.0, jax.random.fold_in(key, 6)
    for dim, parts in pieces:
        heights = jnp.exp(jax.random.uniform(jax.random.fold_in(own, dim), (parts,), jnp.float32, low / len(pieces), top_value / len(pieces)))
        loudness = loudness * jnp.repeat(heights, shape[dim] // parts).reshape([-1 if axis == dim else 1 for axis in range(len(shape))])
    return loudness


def assign_block(own_key, own, number, rows, count, top, reach, lean):
    order = jax.random.permutation(own_key, count)
    heavy_load, common = load_shares(count, rows * top, reach, lean, True), load_shares(count, rows * top, reach, lean, False)
    places = jnp.arange(count)

    def named(sizes, rotation):
        used = int((sizes > 0).sum())
        fixed = max(1, used // 4)
        passed = fixed + (places - fixed + rotation * (used - fixed)) % max(1, count - fixed)
        return jnp.zeros((count,), jnp.int32).at[order[jnp.where(places < fixed, places, passed)]].set(jnp.asarray(sizes, jnp.int32))

    sizes = jnp.where(number % 4 == 0, named(heavy_load, number // 4), named(common, number - number // 4 - 1))
    mixed = jax.random.permutation(jax.random.fold_in(own, 3), count)
    donor, receiver = mixed[0:count // 2 * 2:2], mixed[1:count // 2 * 2:2]
    margin = jnp.minimum(sizes[donor] - 1, reach - sizes[receiver]) // 2
    margin = jnp.where((donor == order[0]) | (receiver == order[0]) | (sizes[receiver] == 0), 0, jnp.maximum(margin, 0))
    passed = jax.random.randint(jax.random.fold_in(own, 4), (count // 2,), 0, 1 << 20) % (margin + 1)
    sizes = sizes.at[donor].add(-passed).at[receiver].add(passed)
    labels = jnp.searchsorted(jnp.cumsum(sizes), jnp.arange(rows * top), side="right").astype(jnp.int32)
    listing = labels.reshape(top, rows).T
    listing = listing[jax.random.permutation(jax.random.fold_in(own, 1), rows)]
    rotation = jax.random.randint(jax.random.fold_in(own, 2), (rows, 1), 0, top)
    return jnp.take_along_axis(listing, (jnp.arange(top)[None, :] + rotation) % top, axis=1)


def load_shares(number_of, total, limit, slope, full):
    portions = [(1 << 20) // math.isqrt(standing ** slope) + 1 for standing in range(1, number_of + 1)]
    largest = limit if full else min(limit, max(-(-total // number_of), total * portions[0] // sum(portions)))
    least = 1 if total - largest >= number_of - 1 else 0
    holding, spare = [largest] + [least] * (number_of - 1), total - largest - least * (number_of - 1)
    while spare > 0:
        movable = [i for i in range(1, number_of) if holding[i] < largest] or [i for i in range(1, number_of) if holding[i] < limit]
        mass, budget = sum([portions[i] for i in movable]), spare
        for i in movable:
            extra = min(limit - holding[i], max(1, budget * portions[i] // mass), spare)
            holding[i] = holding[i] + extra
            spare = spare - extra
    return np.array(holding)


def noise(stream_key, shape, spread, most, shards=(), held_as=jnp.bfloat16):
    values = jax.random.normal(stream_key, shape, jnp.float32) * spread
    if len(shards) > 0:
        values = steps_of(stream_key, shape, shards, -0.22, 0.18) * values
    return jnp.clip(values, min=-most, max=most).astype(held_as)


def setup_inputs(seed: int = 0) -> dict:
    keys = jax.random.split(jax.random.key(seed), 9)
    new_hidden = draw_new_hidden(jax.random.fold_in(keys[8], 71), 0)
    norm_gain = jnp.clip(1.0 + 0.1 * jax.random.normal(keys[1], (D,), jnp.float32), 0.5, 1.5)
    qkv_weight = noise(keys[2], (D, KVH, (GROUP + 2) * HD), D ** -0.5, 0.0625, ((0, 64), (1, 8)))
    out_weight = noise(keys[3], (KVH, GROUP * HD, D), (H * HD) ** -0.5, 0.0625, ((0, 8), (2, 64)))
    owned_cache = draw_owned_cache(jax.random.fold_in(keys[8], 71), 0)
    lengths = draw_lengths(jax.random.fold_in(keys[8], 71), 0)
    owner_device = jax.random.permutation(keys[6], N_CTX).astype(jnp.int32)
    block_target_keys = jax.random.split(jax.random.fold_in(keys[7], 1), (N_CTX * OWN_BLK) // OWN_BLK)
    block_target_turns = jax.random.permutation(jax.random.fold_in(keys[7], 3), (N_CTX * OWN_BLK) // OWN_BLK)
    block_target = jax.vmap(lambda own, number: assign_block(jax.random.fold_in(keys[7], 2), own, number, OWN_BLK, N_CTX, 1, CAP, 2))(block_target_keys, block_target_turns).reshape((N_CTX * OWN_BLK, 1))
    return dict(new_hidden=new_hidden, norm_gain=norm_gain, qkv_weight=qkv_weight, out_weight=out_weight, owned_cache=owned_cache, lengths=lengths, owner_device=owner_device, block_target=block_target)


def rotate(values, position):
    half = values.shape[-1] // 2
    inverse = jnp.exp(-math.log(500000.0) * jnp.arange(half, dtype=jnp.float32) * 2.0 / values.shape[-1])
    angle = position[..., None] * inverse
    cosine = jnp.cos(angle)
    sine = jnp.sin(angle)
    first = values[..., :half]
    second = values[..., half:]
    return jnp.concatenate([first * cosine - second * sine, second * cosine + first * sine], axis=-1)

def reference(new_hidden, norm_gain, qkv_weight, out_weight, owned_cache, lengths, owner_device, block_target):
    targets = block_target[:, 0].reshape(N_CTX, OWN_BLK)
    onehot = (targets[:, :, None] == jnp.arange(N_CTX, dtype=jnp.int32)[None, None, :]).astype(jnp.int32)
    ranking = (lax.optimization_barrier(jnp.sum(jnp.cumsum(onehot, axis=1) * onehot, axis=2)) - 1).astype(jnp.int32)
    sources = jnp.broadcast_to(jnp.arange(N_CTX, dtype=jnp.int32)[:, None], targets.shape)
    blocks = owned_cache.reshape(N_CTX, OWN_BLK, BLOCK, KVH, 2 * HD)
    relaid = jnp.zeros((N_CTX, N_CTX, CAP, BLOCK, KVH, 2 * HD), jnp.bfloat16)
    relaid = relaid.at[targets, sources, ranking].set(blocks)
    relaid = relaid.reshape(N_CTX * N_CTX * CAP, BLOCK, KVH, 2 * HD)
    store = owned_cache.reshape(N_CTX, SEGLEN, KVH, 2 * HD)
    owners = owner_device.reshape(SEQS, SEGS)
    scale = 1.0 / math.sqrt(HD)
    weight_flat = qkv_weight.reshape(D, KVH * (GROUP + 2) * HD)
    out_flat = out_weight.reshape(H * HD, D)
    new_keys = []
    new_values = []
    results = []
    for decode_step in range(STEPS):
        hidden = new_hidden[decode_step]
        scaled = (hidden.astype(jnp.float32) * norm_gain).astype(jnp.bfloat16)
        projected = jnp.dot(scaled, weight_flat, preferred_element_type=jnp.float32)
        squares = lax.optimization_barrier(jnp.sum(jnp.square(hidden.astype(jnp.float32)), axis=1))
        projected = projected / jnp.sqrt(squares / D + 1e-05)[:, None]
        projected = projected.reshape(SEQS, KVH, GROUP + 2, HD)
        position = lengths.astype(jnp.float32) + decode_step
        queries = rotate(projected[:, :, :GROUP], position[:, None, None]).astype(jnp.bfloat16)
        new_keys.append(rotate(projected[:, :, GROUP], position[:, None]).astype(jnp.bfloat16))
        new_values.append(projected[:, :, GROUP + 1].astype(jnp.bfloat16))
        fresh_keys = jnp.stack(new_keys, 2)
        fresh_values = jnp.stack(new_values, 2)

        def one_sequence(record):
            query_rows, owner_row, length, keys_new, values_new = record
            cache = jnp.take(store, owner_row, axis=0).reshape(MAXLEN, KVH, 2 * HD)
            query_wide = query_rows.astype(jnp.float32)
            scores = jnp.einsum('kgd,jkd->kgj', query_wide, cache[..., :HD].astype(jnp.float32)) * scale
            live_mask = jnp.arange(MAXLEN, dtype=jnp.int32) < length
            scores = jnp.where(live_mask[None, None, :], scores, -1e+30)
            fresh_scores = jnp.einsum('kgd,ktd->kgt', query_wide, keys_new.astype(jnp.float32)) * scale
            highest = jnp.maximum(lax.optimization_barrier(jnp.max(scores, axis=-1)), lax.optimization_barrier(jnp.max(fresh_scores, axis=-1)))
            weights = jnp.where(live_mask[None, None, :], jnp.exp(scores - highest[..., None]), 0.0)
            fresh_weights = jnp.exp(fresh_scores - highest[..., None])
            total = lax.optimization_barrier(jnp.sum(weights, axis=-1)) + lax.optimization_barrier(jnp.sum(fresh_weights, axis=-1))
            weights_low = lax.optimization_barrier(weights.astype(jnp.bfloat16)).astype(jnp.float32)
            fresh_low = lax.optimization_barrier(fresh_weights.astype(jnp.bfloat16)).astype(jnp.float32)
            accumulated = jnp.einsum('kgj,jkd->kgd', weights_low, cache[..., HD:].astype(jnp.float32))
            accumulated = accumulated + jnp.einsum('kgt,ktd->kgd', fresh_low, values_new.astype(jnp.float32))
            return (accumulated / total[..., None]).astype(jnp.bfloat16)
        attention = lax.map(one_sequence, (queries, owners, lengths, fresh_keys, fresh_values))
        mixed = jnp.dot(attention.reshape(SEQS, H * HD), out_flat, preferred_element_type=jnp.float32)
        results.append(mixed.astype(jnp.bfloat16))
    return (jnp.stack(results, 0), relaid)
```

```python
import functools
import math

import jax
import jax.numpy as jnp
import numpy as np
from jax import lax
from jax.experimental import pallas as pl
from jax.experimental.pallas import tpu as pltpu
from jax.sharding import PartitionSpec as P

MESH = pl.DeviceIdType.MESH
ZN, XN, TP = 16, 4, 8
HEADS = 8
LOW = -1e30


def remote(src, dst, send, recv, target):
    return pltpu.make_async_remote_copy(
        src_ref=src,
        dst_ref=dst,
        send_sem=send,
        recv_sem=recv,
        device_id=target,
        device_id_type=MESH,
    )


def wait_bytes(ref, sem):
    pltpu.make_async_copy(ref, ref, sem).wait()


def swap_halves(values, axis):
    return pltpu.roll(values, 64, axis)


def kernel(
    hid_ref, gain_ref, inv_ref, len_ref, own_ref, tgt_hbm, wq_hbm, wo_hbm, cache_hbm,
    att_ref, rel_ref,
    tgt, slot_v, slot_s, wq, wo, cache, packed,
    hid32, pbuf, zbuf, xsend, xbuf, asend, gbuf, kvs,
    bbuf, zb2, x2send, x2buf, ats, agb, osend, tbuf, fs,
    in_sem, own_sem, a2a_send, a2a_recv, chain_send, chain_recv,
):
    me = lax.axis_index("ctx")
    mt = lax.axis_index("tp")
    z = me // XN
    x = me % XN

    def at_z(dz):
        return ((z + dz) % ZN) * XN + x

    def at_x(dx):
        return z * XN + (x + dx) % XN

    barrier = pltpu.get_barrier_semaphore()

    def greet_ctx(k, carry):
        pl.semaphore_signal(barrier, inc=1, device_id={"ctx": (me + k) % (ZN * XN)}, device_id_type=MESH)
        return carry

    def greet_tp(k, carry):
        pl.semaphore_signal(barrier, inc=1, device_id={"tp": (mt + k) % TP}, device_id_type=MESH)
        return carry

    lax.fori_loop(1, ZN * XN, greet_ctx, 0)
    lax.fori_loop(1, TP, greet_tp, 0)

    cp_tgt = pltpu.make_async_copy(tgt_hbm.at[me], tgt, in_sem.at[0])
    cp_wq = pltpu.make_async_copy(wq_hbm, wq, in_sem.at[1])
    cp_cache = pltpu.make_async_copy(cache_hbm, cache, in_sem.at[2])
    cp_wo = pltpu.make_async_copy(wo_hbm, wo, in_sem.at[3])
    cp_tgt.start()
    cp_wq.start()
    cp_cache.start()
    cp_wo.start()

    hid32[...] = jnp.zeros_like(hid32)
    for step in range(3):
        hid32[4 * step : 4 * step + 4, :] = hid_ref[step].astype(jnp.float32)
    hidden = hid32[...]
    scaled = (hidden * gain_ref[...]).astype(jnp.bfloat16)
    row16 = lax.broadcasted_iota(jnp.int32, (16, 128), 0)
    lane16 = lax.broadcasted_iota(jnp.int32, (16, 128), 1)
    squares = jnp.sum(hidden * hidden, axis=1, keepdims=True)
    square_row = jnp.sum(jnp.where(row16 == lane16, squares, 0.0), axis=0, keepdims=True)
    row8 = lax.broadcasted_iota(jnp.int32, (8, 128), 0)
    lane8 = lax.broadcasted_iota(jnp.int32, (8, 128), 1)
    pbuf[120:128, :] = jnp.where(row8 == 0, square_row, 0.0)
    cp_wq.wait()
    for head in range(HEADS + 2):
        part = jnp.dot(
            scaled, wq[:, 128 * head : 128 * head + 128], preferred_element_type=jnp.float32
        )
        pbuf[12 * head : 12 * head + 12, :] = part[0:12, :]

    cp_tgt.wait()
    t_iota = lax.broadcasted_iota(jnp.int32, (64, 128), 0)
    b_iota = lax.broadcasted_iota(jnp.int32, (64, 128), 1)
    match = tgt[...] == t_iota
    first = jnp.min(jnp.where(match, b_iota, 127), axis=1, keepdims=True)
    last = jnp.max(jnp.where(match, b_iota, 0), axis=1, keepdims=True)
    slot_v[...] = jnp.where(b_iota == 0, first, last)
    cp_slot = pltpu.make_async_copy(slot_v, slot_s, in_sem.at[4])
    cp_slot.start()
    cp_slot.wait()
    cp_cache.wait()

    def pack(t, carry):
        packed[2 * t] = cache[slot_s[t, 0]]
        packed[2 * t + 1] = cache[slot_s[t, 1]]
        return carry

    lax.fori_loop(0, ZN * XN, pack, 0)
    mine = pl.ds(2 * me, 2)
    cp_own = pltpu.make_async_copy(packed.at[mine], rel_ref.at[mine], own_sem)
    cp_own.start()

    row24 = lax.broadcasted_iota(jnp.int32, (24, 128), 0)
    lane24 = lax.broadcasted_iota(jnp.int32, (24, 128), 1)
    seq24 = row24 % 4
    row_in = row24 % 12
    length24 = jnp.where(
        seq24 == 0,
        len_ref[0],
        jnp.where(seq24 == 1, len_ref[1], jnp.where(seq24 == 2, len_ref[2], len_ref[3])),
    )
    position = length24.astype(jnp.float32) + (row_in // 4).astype(jnp.float32)
    angle = position * inv_ref[...]
    cosine = jnp.cos(angle)
    sine = jnp.where(lane24 < 64, -jnp.sin(angle), jnp.sin(angle))

    own_iota = lax.broadcasted_iota(jnp.int32, (1, 64), 1)
    segment = jnp.sum(jnp.where(own_ref[...] == me, own_iota, 0), axis=1, keepdims=True)
    my_seq = segment // 16
    my_offset = segment % 16 * 2048
    my_length = jnp.where(
        my_seq == 0,
        len_ref[0],
        jnp.where(my_seq == 1, len_ref[1], jnp.where(my_seq == 2, len_ref[2], len_ref[3])),
    )

    pl.semaphore_wait(barrier, ZN * XN - 1 + TP - 1)

    def send_blocks(dzs, low, high):
        def one(dx, carry):
            for dz in dzs:
                to = ((z + dz + ZN) % ZN) * XN + (x + dx) % XN
                remote(
                    packed.at[pl.ds(2 * to, 2)], rel_ref.at[mine], a2a_send, a2a_recv, {"ctx": to}
                ).start()
            return carry

        lax.fori_loop(low, high, one, 0)

    def scatter_a(dz, carry):
        to = (z + dz) % ZN
        remote(
            pbuf.at[pl.ds(pl.multiple_of(8 * to, 8), 8)], zbuf.at[z],
            chain_send.at[0], chain_recv.at[0], {"ctx": to * XN + x},
        ).start()
        return carry

    lax.fori_loop(1, ZN, scatter_a, 0)
    send_blocks(A2A_PLAN[0][0], *A2A_PLAN[0][1])
    zbuf[z] = pbuf[pl.ds(pl.multiple_of(8 * z, 8), 8), :]
    wait_bytes(zbuf.at[pl.ds(0, ZN - 1)], chain_recv.at[0])
    total = jnp.sum(zbuf[...], axis=0)
    xsend[...] = total
    xbuf[x] = total
    for dx in range(1, XN):
        remote(
            xsend, xbuf.at[x], chain_send.at[1], chain_recv.at[1], {"ctx": at_x(dx)}
        ).start()
    wait_bytes(xbuf.at[pl.ds(0, XN - 1)], chain_recv.at[1])
    total = jnp.sum(xbuf[...], axis=0)
    asend[...] = total
    gbuf[z] = total

    def gather_a(dz, carry):
        remote(
            asend, gbuf.at[z], chain_send.at[2], chain_recv.at[2], {"ctx": at_z(dz)}
        ).start()
        return carry

    lax.fori_loop(1, ZN, gather_a, 0)
    send_blocks(A2A_PLAN[1][0], *A2A_PLAN[1][1])
    wait_bytes(gbuf.at[pl.ds(0, ZN - 1)], chain_recv.at[2])

    whole = gbuf[...].reshape(128, 128)
    square_sum = jnp.sum(
        jnp.where(lane24 == row_in, whole[120:121, :], 0.0), axis=1, keepdims=True
    )
    norm = jnp.sqrt(square_sum / 8192.0 + 1e-05)
    rotated = []
    for g in range(5):
        plain = whole[24 * g : 24 * g + 24, :] / norm
        turned = plain * cosine + swap_halves(plain, 1) * sine
        if g < 4:
            rotated.append(turned)
        else:
            kvs[0:24, :] = jnp.where(row24 < 12, turned, plain)
    kvs[24:32, :] = jnp.zeros((8, 128), jnp.float32)
    queries = jnp.concatenate(rotated, axis=0).astype(jnp.bfloat16)

    pick_row = lax.broadcasted_iota(jnp.int32, (64, 96), 0)
    pick_col = lax.broadcasted_iota(jnp.int32, (64, 96), 1)
    in_tile = pick_row % 8
    tile_step = jnp.where(in_tile >= 3, in_tile - 3, in_tile)
    wanted = 12 * (pick_row // 8) + 4 * tile_step + my_seq
    pick = jnp.where((wanted == pick_col) & (in_tile < 6), 1.0, 0.0).astype(jnp.bfloat16)
    my_queries = jnp.dot(pick, queries, preferred_element_type=jnp.float32).astype(jnp.bfloat16)
    keys = cache[:, :, 0:128].reshape(2048, 128)
    values = cache[:, :, 128:256].reshape(2048, 128)
    scale = 1.0 / math.sqrt(128)
    scores = (
        lax.dot_general(
            my_queries, keys, (((1,), (1,)), ((), ())), preferred_element_type=jnp.float32
        )
        * scale
    )
    place = my_offset + lax.broadcasted_iota(jnp.int32, (1, 2048), 1)
    live = place < my_length
    scores = jnp.where(live, scores, LOW)
    highest = jnp.max(scores, axis=1, keepdims=True)
    weights = jnp.where(live, jnp.exp(scores - highest), 0.0)
    weight_sum = jnp.sum(weights, axis=1, keepdims=True)
    weighted = jnp.dot(weights.astype(jnp.bfloat16), values, preferred_element_type=jnp.float32)
    row64 = lax.broadcasted_iota(jnp.int32, (64, 128), 0) % 8
    lane64 = lax.broadcasted_iota(jnp.int32, (64, 128), 1)
    stats = jnp.where(lane64 < 64, highest, weight_sum)
    bbuf[...] = jnp.where(
        row64 < 3, weighted, jnp.where(row64 < 6, stats, my_seq.astype(jnp.float32))
    )

    head = z % HEADS

    def scatter_b(dz, carry):
        to = (z + dz) % ZN
        remote(
            bbuf.at[pl.ds(pl.multiple_of(8 * (to % HEADS), 8), 8)], zb2.at[z],
            chain_send.at[3], chain_recv.at[3], {"ctx": to * XN + x},
        ).start()
        return carry

    lax.fori_loop(1, ZN, scatter_b, 0)
    send_blocks(A2A_PLAN[2][0], *A2A_PLAN[2][1])
    zb2[z] = bbuf[pl.ds(pl.multiple_of(8 * head, 8), 8), :]

    pick_row = lax.broadcasted_iota(jnp.int32, (16, 96), 0)
    pick_col = lax.broadcasted_iota(jnp.int32, (16, 96), 1)
    wanted = 12 * head + 4 * (pick_row % 3) + pick_row // 3
    pick = jnp.where((wanted == pick_col) & (pick_row < 12), 1.0, 0.0).astype(jnp.bfloat16)
    head_queries = jnp.dot(pick, queries, preferred_element_type=jnp.float32).astype(jnp.bfloat16)
    new_keys = kvs[0:16, :].astype(jnp.bfloat16)
    new_values = kvs[12:28, :].astype(jnp.bfloat16)
    fresh = (
        lax.dot_general(
            head_queries, new_keys, (((1,), (1,)), ((), ())), preferred_element_type=jnp.float32
        )
        * scale
    )
    q_row = lax.broadcasted_iota(jnp.int32, (16, 16), 0)
    k_col = lax.broadcasted_iota(jnp.int32, (16, 16), 1)
    seen = (
        (q_row // 3 == k_col % 4) & (k_col // 4 <= q_row % 3) & (k_col < 12) & (q_row < 12)
    )
    fresh = jnp.where(seen, fresh, LOW)
    fresh_high = jnp.max(fresh, axis=1, keepdims=True)
    x2send[...] = jnp.where(lax.broadcasted_iota(jnp.int32, (32, 128), 0) < 16, 0.0, 1.0)

    wait_bytes(zb2.at[pl.ds(0, ZN - 1)], chain_recv.at[3])
    tiles = zb2[...]
    lane_t = lax.broadcasted_iota(jnp.int32, (16, 8, 128), 2)
    moved = pltpu.roll(tiles, 5, 1)
    turned = swap_halves(moved, 2)
    part_high = jnp.where(lane_t < 64, moved, turned)
    part_sum = jnp.where(lane_t < 64, turned, moved)
    part_seq = tiles[:, 6:7, :]
    for seq in range(4):
        member = part_seq == float(seq)
        high = jnp.max(jnp.where(member, part_high, LOW), axis=0)
        factor = jnp.where(member, jnp.exp(part_high - high[None]), 0.0)
        sums = jnp.sum(factor * part_sum, axis=0)
        accs = jnp.sum(factor * tiles, axis=0)
        both = jnp.where(lane8 < 64, high, sums)
        x2send[3 * seq : 3 * seq + 3, :] = accs[0:3, :]
        x2send[16 + 3 * seq : 16 + 3 * seq + 3, :] = both[0:3, :]
    x2buf[x] = x2send[...]
    for dx in range(1, XN):
        remote(
            x2send, x2buf.at[x], chain_send.at[4], chain_recv.at[4], {"ctx": at_x(dx)}
        ).start()
    send_blocks(A2A_PLAN[3][0], *A2A_PLAN[3][1])
    wait_bytes(x2buf.at[pl.ds(0, XN - 1)], chain_recv.at[4])
    accs = x2buf[:, 0:16, :]
    stats = x2buf[:, 16:32, :]
    lane_x = lax.broadcasted_iota(jnp.int32, (4, 16, 128), 2)
    turned = swap_halves(stats, 2)
    part_high = jnp.where(lane_x < 64, stats, turned)
    part_sum = jnp.where(lane_x < 64, turned, stats)
    high = jnp.maximum(jnp.max(part_high, axis=0), fresh_high)
    factor = jnp.exp(part_high - high[None])
    fresh_weights = jnp.where(seen, jnp.exp(fresh - high[:, 0:1]), 0.0)
    sums = jnp.sum(factor * part_sum, axis=0) + jnp.sum(fresh_weights, axis=1, keepdims=True)
    mixed = jnp.sum(factor * accs, axis=0) + jnp.dot(
        fresh_weights.astype(jnp.bfloat16), new_values, preferred_element_type=jnp.float32
    )
    attention = (mixed / sums).astype(jnp.bfloat16)
    ats[...] = attention
    agb[head] = attention
    for dz in (1, -1, 2, -2, 3, -3, 4):
        remote(
            ats, agb.at[head], chain_send.at[5], chain_recv.at[5], {"ctx": at_z(dz + ZN)}
        ).start()
    send_blocks(A2A_PLAN[4][0], *A2A_PLAN[4][1])
    cp_wo.wait()
    wait_bytes(agb.at[pl.ds(0, HEADS - 1)], chain_recv.at[5])

    out = jnp.zeros((16, 128), jnp.float32)
    for h in range(HEADS):
        out = out + jnp.dot(
            agb[h], wo[128 * h : 128 * h + 128, :], preferred_element_type=jnp.float32
        )
    osend[...] = out
    tbuf[mt] = out
    for dt in range(1, TP):
        remote(
            osend, tbuf.at[mt], chain_send.at[6], chain_recv.at[6], {"tp": (mt + dt) % TP}
        ).start()
    send_blocks(A2A_PLAN[5][0], *A2A_PLAN[5][1])
    wait_bytes(tbuf.at[pl.ds(0, TP - 1)], chain_recv.at[6])
    out = jnp.sum(tbuf[...], axis=0)
    for step in range(3):
        for seq in range(4):
            r = 3 * seq + step
            fs[step, seq : seq + 1, :] = out[r : r + 1, :]
    att_ref[...] = fs[...].astype(jnp.bfloat16)

    wait_bytes(pbuf.at[pl.ds(0, 8 * (ZN - 1))], chain_send.at[0])
    wait_bytes(xbuf.at[pl.ds(0, XN - 1)], chain_send.at[1])
    wait_bytes(gbuf.at[pl.ds(0, ZN - 1)], chain_send.at[2])
    wait_bytes(zb2.at[pl.ds(0, ZN - 1)], chain_send.at[3])
    wait_bytes(x2buf.at[pl.ds(0, XN - 1)], chain_send.at[4])
    wait_bytes(agb.at[pl.ds(0, HEADS - 1)], chain_send.at[5])
    wait_bytes(tbuf.at[pl.ds(0, TP - 1)], chain_send.at[6])
    cp_own.wait()
    others = pl.ds(0, 2 * (ZN * XN - 1))
    wait_bytes(packed.at[others], a2a_send)
    wait_bytes(rel_ref.at[others], a2a_recv)


A2A_PLAN = (
    ((1, -1, 7, -7), (0, 4)),
    ((2, -2, 6, -6), (0, 4)),
    ((3, -3, 5, -5), (0, 4)),
    ((4, -4, 8), (0, 4)),
    ((0,), (1, 4)),
    ((), (0, 0)),
)


def inverse_table():
    half = np.arange(64, dtype=np.float32)
    power = np.float32(-math.log(500000.0)) * half * np.float32(2.0) / np.float32(128.0)
    inverse = np.exp(power.astype(np.float64)).astype(np.float32)
    return np.concatenate([inverse, inverse])[None, :]


def body(
    new_hidden, norm_gain, qkv_weight, out_weight, owned_cache, lengths, owner_device, block_target
):
    f32, bf16, i32 = jnp.float32, jnp.bfloat16, jnp.int32
    vmem = pl.BlockSpec(memory_space=pltpu.VMEM)
    smem = pl.BlockSpec(memory_space=pltpu.SMEM)
    hbm = pl.BlockSpec(memory_space=pl.ANY)
    dma = pltpu.SemaphoreType.DMA
    attended, relaid = pl.pallas_call(
        kernel,
        out_shape=(
            jax.ShapeDtypeStruct((3, 4, 128), bf16),
            jax.ShapeDtypeStruct((128, 16, 256), bf16),
        ),
        in_specs=[vmem, vmem, vmem, smem, vmem, hbm, hbm, hbm, hbm],
        out_specs=(vmem, hbm),
        scratch_shapes=[
            pltpu.VMEM((1, 128), i32),
            pltpu.VMEM((64, 128), i32),
            pltpu.SMEM((64, 128), i32),
            pltpu.VMEM((128, 1280), bf16),
            pltpu.VMEM((1024, 128), bf16),
            pltpu.VMEM((128, 16, 256), bf16),
            pltpu.VMEM((128, 16, 256), bf16),
            pltpu.VMEM((16, 128), f32),
            pltpu.VMEM((128, 128), f32),
            pltpu.VMEM((16, 8, 128), f32),
            pltpu.VMEM((8, 128), f32),
            pltpu.VMEM((4, 8, 128), f32),
            pltpu.VMEM((8, 128), f32),
            pltpu.VMEM((16, 8, 128), f32),
            pltpu.VMEM((32, 128), f32),
            pltpu.VMEM((64, 128), f32),
            pltpu.VMEM((16, 8, 128), f32),
            pltpu.VMEM((32, 128), f32),
            pltpu.VMEM((4, 32, 128), f32),
            pltpu.VMEM((16, 128), bf16),
            pltpu.VMEM((8, 16, 128), bf16),
            pltpu.VMEM((16, 128), f32),
            pltpu.VMEM((8, 16, 128), f32),
            pltpu.VMEM((3, 4, 128), f32),
            dma((5,)),
            dma,
            dma,
            dma,
            dma((7,)),
            dma((7,)),
        ],
        compiler_params=pltpu.CompilerParams(
            collective_id=0, has_side_effects=True, vmem_limit_bytes=32 * 1024 * 1024
        ),
        name="decode_and_relay",
    )(
        new_hidden,
        norm_gain.reshape(1, 128),
        jnp.asarray(inverse_table()),
        lengths,
        owner_device.reshape(1, 64),
        block_target.reshape(64, 1, 128),
        qkv_weight.reshape(128, 1280),
        out_weight.reshape(1024, 128),
        owned_cache.reshape(128, 16, 256),
    )
    return attended, relaid.reshape(128, 16, 1, 256)


def solution(mesh):
    in_specs = (
        P(None, None, "ctx"),
        P("ctx"),
        P("ctx", "tp", None),
        P("tp", None, "ctx"),
        P("ctx", None, "tp", None),
        P(),
        P(),
        P(),
    )
    out_specs = (P(None, None, "ctx"), P("ctx", None, "tp", None))
    return jax.shard_map(body, mesh=mesh, in_specs=in_specs, out_specs=out_specs, check_vma=False)
```

```python
import functools
import math

import jax
import jax.numpy as jnp
import numpy as np
from jax import lax
from jax.experimental import pallas as pl
from jax.experimental.pallas import tpu as pltpu
from jax.sharding import PartitionSpec as P

MESH = pl.DeviceIdType.MESH
ZN, XN, TP = 16, 4, 8
HEADS = 8
LOW = -1e30
VL = 60


def remote(src, dst, send, recv, target):
    return pltpu.make_async_remote_copy(
        src_ref=src,
        dst_ref=dst,
        send_sem=send,
        recv_sem=recv,
        device_id=target,
        device_id_type=MESH,
    )


def wait_bytes(ref, sem):
    pltpu.make_async_copy(ref, ref, sem).wait()


def swap_halves(values, axis):
    return pltpu.roll(values, 64, axis)


def kernel(
    len_ref, hid_hbm, gain_hbm, inv_hbm, own_hbm, tgt_hbm, wq_hbm, wo_hbm, cache_hbm,
    att_ref, rel_ref,
    hid_ref, gain_ref, inv_ref, own_ref, tgt, slot_v, slot_s, wq, wo, cache, packed,
    hid32, pbuf, xbuf, zsend, zbuf, asend, gz, xsend, gbuf, kvs,
    bbuf, zb2, x2send, x2buf, ats, agb, osend, tbuf, fs,
    in_sem, own_sem, a2a_send, a2a_recv, chain_send, chain_recv,
):
    me = lax.axis_index("ctx")
    mt = lax.axis_index("tp")
    z = me // XN
    x = me % XN

    def at_z(dz):
        return ((z + dz) % ZN) * XN + x

    def at_x(dx):
        return z * XN + (x + dx) % XN

    barrier = pltpu.get_barrier_semaphore()

    def greet_ctx(k, carry):
        pl.semaphore_signal(barrier, inc=1, device_id={"ctx": (me + k) % (ZN * XN)}, device_id_type=MESH)
        return carry

    def greet_tp(k, carry):
        pl.semaphore_signal(barrier, inc=1, device_id={"tp": (mt + k) % TP}, device_id_type=MESH)
        return carry

    lax.fori_loop(1, ZN * XN, greet_ctx, 0)
    lax.fori_loop(1, TP, greet_tp, 0)

    cp_tgt = pltpu.make_async_copy(tgt_hbm.at[me], tgt, in_sem.at[0])
    cp_wq = pltpu.make_async_copy(wq_hbm, wq, in_sem.at[1])
    cp_cache = pltpu.make_async_copy(cache_hbm, cache, in_sem.at[2])
    cp_wo = pltpu.make_async_copy(wo_hbm, wo, in_sem.at[3])
    cp_hid = pltpu.make_async_copy(hid_hbm, hid_ref, in_sem.at[5])
    cp_gain = pltpu.make_async_copy(gain_hbm, gain_ref, in_sem.at[6])
    cp_inv = pltpu.make_async_copy(inv_hbm, inv_ref, in_sem.at[7])
    cp_own_dev = pltpu.make_async_copy(own_hbm, own_ref, in_sem.at[8])
    cp_tgt.start()
    cp_hid.start()
    cp_gain.start()
    cp_wq.start()
    cp_cache.start()
    cp_inv.start()
    cp_own_dev.start()
    cp_wo.start()

    hid32[...] = jnp.zeros_like(hid32)
    cp_hid.wait()
    cp_gain.wait()
    for step in range(3):
        hid32[4 * step : 4 * step + 4, :] = hid_ref[step].astype(jnp.float32)
    hidden = hid32[...]
    scaled = (hidden * gain_ref[...]).astype(jnp.bfloat16)
    row16 = lax.broadcasted_iota(jnp.int32, (16, 128), 0)
    lane16 = lax.broadcasted_iota(jnp.int32, (16, 128), 1)
    squares = jnp.sum(hidden * hidden, axis=1, keepdims=True)
    square_row = jnp.sum(jnp.where(row16 == lane16, squares, 0.0), axis=0, keepdims=True)
    row8 = lax.broadcasted_iota(jnp.int32, (8, 128), 0)
    lane8 = lax.broadcasted_iota(jnp.int32, (8, 128), 1)
    pbuf[120:128, :] = jnp.where(row8 == 0, square_row, 0.0)
    cp_wq.wait()
    for head in range(HEADS + 2):
        part = jnp.dot(
            scaled, wq[:, 128 * head : 128 * head + 128], preferred_element_type=jnp.float32
        )
        pbuf[12 * head : 12 * head + 12, :] = part[0:12, :]

    cp_tgt.wait()
    t_iota = lax.broadcasted_iota(jnp.int32, (64, 128), 0)
    b_iota = lax.broadcasted_iota(jnp.int32, (64, 128), 1)
    match = tgt[...] == t_iota
    first = jnp.min(jnp.where(match, b_iota, 127), axis=1, keepdims=True)
    last = jnp.max(jnp.where(match, b_iota, 0), axis=1, keepdims=True)
    slot_v[...] = jnp.where(b_iota == 0, first, last)
    cp_slot = pltpu.make_async_copy(slot_v, slot_s, in_sem.at[4])
    cp_slot.start()
    cp_slot.wait()
    cp_cache.wait()

    def pack(t, carry):
        packed[2 * t] = cache[slot_s[t, 0]]
        packed[2 * t + 1] = cache[slot_s[t, 1]]
        return carry

    lax.fori_loop(0, ZN * XN, pack, 0)
    mine = pl.ds(2 * me, 2)
    cp_own = pltpu.make_async_copy(packed.at[mine], rel_ref.at[mine], own_sem)
    cp_own.start()

    row24 = lax.broadcasted_iota(jnp.int32, (24, 128), 0)
    lane24 = lax.broadcasted_iota(jnp.int32, (24, 128), 1)
    seq24 = row24 % 4
    row_in = row24 % 12
    length24 = jnp.where(
        seq24 == 0,
        len_ref[0],
        jnp.where(seq24 == 1, len_ref[1], jnp.where(seq24 == 2, len_ref[2], len_ref[3])),
    )
    position = length24.astype(jnp.float32) + (row_in // 4).astype(jnp.float32)
    cp_inv.wait()
    angle = position * inv_ref[...]
    cosine = jnp.cos(angle)
    sine = jnp.where(lane24 < 64, -jnp.sin(angle), jnp.sin(angle))

    cp_own_dev.wait()
    own_iota = lax.broadcasted_iota(jnp.int32, (1, 64), 1)
    segment = jnp.sum(jnp.where(own_ref[...] == me, own_iota, 0), axis=1, keepdims=True)
    my_seq = segment // 16
    my_offset = segment % 16 * 2048
    my_length = jnp.where(
        my_seq == 0,
        len_ref[0],
        jnp.where(my_seq == 1, len_ref[1], jnp.where(my_seq == 2, len_ref[2], len_ref[3])),
    )

    pl.semaphore_wait(barrier, ZN * XN - 1 + TP - 1)

    def send_blocks(dz, dx):
        to = ((z + dz + ZN) % ZN) * XN + (x + dx) % XN
        remote(
            packed.at[pl.ds(2 * to, 2)], rel_ref.at[mine], a2a_send, a2a_recv, {"ctx": to}
        ).start()

    def bulk(slot):
        for odd, dx in PLAN[slot]:

            def both_ways(step, carry):
                dz = 2 * step + 1 if odd else 2 * step
                send_blocks(dz, dx)
                send_blocks(-dz, dx)
                return carry

            if odd:
                lax.fori_loop(0, 4, both_ways, 0)
            else:
                send_blocks(8, dx)
                lax.fori_loop(1, 4, both_ways, 0)
                if dx > 0:
                    send_blocks(0, dx)

    quarter = pl.ds(pl.multiple_of(32 * x, 32), 32)
    for dx in range(1, XN):
        to = (x + dx) % XN
        remote(
            pbuf.at[pl.ds(pl.multiple_of(32 * to, 32), 32)], xbuf.at[x],
            chain_send.at[0], chain_recv.at[0], {"ctx": at_x(dx)},
        ).start()
    bulk(0)
    xbuf[x] = pbuf[quarter, :]
    wait_bytes(xbuf.at[pl.ds(0, XN - 1)], chain_recv.at[0])
    total = jnp.sum(xbuf[...], axis=0)
    for c in range(8):
        zsend[c] = total[4 * c : 4 * c + 4, :]
    chunk = z % 8

    def scatter_a(dz, carry):
        to = (z + dz) % ZN
        remote(
            zsend.at[to % 8], zbuf.at[z], chain_send.at[1], chain_recv.at[1], {"ctx": to * XN + x}
        ).start()
        return carry

    lax.fori_loop(1, ZN, scatter_a, 0)
    bulk(1)
    zbuf[z] = zsend[chunk]
    wait_bytes(zbuf.at[pl.ds(0, ZN - 1)], chain_recv.at[1])
    total = jnp.sum(zbuf[...], axis=0)
    asend[...] = total
    gz[chunk] = total
    for dz in (1, -1, 2, -2, 3, -3, 4):
        remote(
            asend, gz.at[chunk], chain_send.at[2], chain_recv.at[2], {"ctx": at_z(dz + ZN)}
        ).start()
    bulk(2)
    wait_bytes(gz.at[pl.ds(0, 7)], chain_recv.at[2])
    for c in range(8):
        xsend[4 * c : 4 * c + 4, :] = gz[c]
    for dx in range(1, XN):
        remote(
            xsend, gbuf.at[x], chain_send.at[3], chain_recv.at[3], {"ctx": at_x(dx)}
        ).start()
    bulk(3)
    gbuf[x] = xsend[...]
    wait_bytes(gbuf.at[pl.ds(0, XN - 1)], chain_recv.at[3])

    whole = gbuf[...].reshape(128, 128)
    square_sum = jnp.sum(
        jnp.where(lane24 == row_in, whole[120:121, :], 0.0), axis=1, keepdims=True
    )
    norm = jnp.sqrt(square_sum / 8192.0 + 1e-05)
    rotated = []
    for g in range(5):
        plain = whole[24 * g : 24 * g + 24, :] / norm
        turned = plain * cosine + swap_halves(plain, 1) * sine
        if g < 4:
            rotated.append(turned)
        else:
            kvs[0:24, :] = jnp.where(row24 < 12, turned, plain)
    kvs[24:32, :] = jnp.zeros((8, 128), jnp.float32)
    queries = jnp.concatenate(rotated, axis=0).astype(jnp.bfloat16)

    pick_row = lax.broadcasted_iota(jnp.int32, (32, 96), 0)
    pick_col = lax.broadcasted_iota(jnp.int32, (32, 96), 1)
    wanted = 12 * (pick_row // 4) + 4 * (pick_row % 4) + my_seq
    pick = jnp.where((wanted == pick_col) & (pick_row % 4 < 3), 1.0, 0.0).astype(jnp.bfloat16)
    my_queries = jnp.dot(pick, queries, preferred_element_type=jnp.float32).astype(jnp.bfloat16)
    keys = cache[:, :, 0:128].reshape(2048, 128)
    values = cache[:, :, 128:256].reshape(2048, 128)
    scale = 1.0 / math.sqrt(128)
    scores = (
        lax.dot_general(
            my_queries, keys, (((1,), (1,)), ((), ())), preferred_element_type=jnp.float32
        )
        * scale
    )
    place = my_offset + lax.broadcasted_iota(jnp.int32, (1, 2048), 1)
    live = place < my_length
    scores = jnp.where(live, scores, LOW)
    highest = jnp.max(scores, axis=1, keepdims=True)
    weights = jnp.where(live, jnp.exp(scores - highest), 0.0)
    weight_sum = jnp.sum(weights, axis=1, keepdims=True)
    weighted = jnp.dot(weights.astype(jnp.bfloat16), values, preferred_element_type=jnp.float32)
    row32 = lax.broadcasted_iota(jnp.int32, (32, 128), 0) % 4
    lane32 = lax.broadcasted_iota(jnp.int32, (32, 128), 1)
    stats = jnp.where(lane32 < 3, highest, weight_sum)
    placed = my_seq.astype(jnp.float32)
    for step in range(3):
        shifted = pltpu.roll(stats, 3 - step, 0)
        placed = jnp.where((lane32 == step) | (lane32 == 3 + step), shifted, placed)
    partial = jnp.where(row32 < 3, weighted, placed)
    for h in range(HEADS):
        bbuf[h] = partial[4 * h : 4 * h + 4, :]

    head = z % HEADS

    def scatter_b(dz, carry):
        to = (z + dz) % ZN
        remote(
            bbuf.at[to % HEADS], zb2.at[z], chain_send.at[4], chain_recv.at[4], {"ctx": to * XN + x}
        ).start()
        return carry

    lax.fori_loop(1, ZN, scatter_b, 0)
    bulk(4)
    zb2[z] = bbuf[head]

    pick_row = lax.broadcasted_iota(jnp.int32, (16, 96), 0)
    pick_col = lax.broadcasted_iota(jnp.int32, (16, 96), 1)
    wanted = 12 * head + 4 * (pick_row % 3) + pick_row // 3
    pick = jnp.where((wanted == pick_col) & (pick_row < 12), 1.0, 0.0).astype(jnp.bfloat16)
    head_queries = jnp.dot(pick, queries, preferred_element_type=jnp.float32).astype(jnp.bfloat16)
    new_keys = kvs[0:16, :].astype(jnp.bfloat16)
    new_values = kvs[12:28, :].astype(jnp.bfloat16)
    fresh = (
        lax.dot_general(
            head_queries, new_keys, (((1,), (1,)), ((), ())), preferred_element_type=jnp.float32
        )
        * scale
    )
    q_row = lax.broadcasted_iota(jnp.int32, (16, 16), 0)
    k_col = lax.broadcasted_iota(jnp.int32, (16, 16), 1)
    seen = (
        (q_row // 3 == k_col % 4) & (k_col // 4 <= q_row % 3) & (k_col < 12) & (q_row < 12)
    )
    fresh = jnp.where(seen, fresh, LOW)
    fresh_high = jnp.max(fresh, axis=1, keepdims=True)
    x2send[...] = jnp.where(lax.broadcasted_iota(jnp.int32, (32, 128), 0) < 16, 0.0, 1.0)

    wait_bytes(zb2.at[pl.ds(0, ZN - 1)], chain_recv.at[4])
    stats = zb2[:, 3, :]
    part_sum = pltpu.roll(stats, 125, 1)
    part_seq = stats[:, 6:7]
    lane1 = lax.broadcasted_iota(jnp.int32, (1, 128), 1)
    for seq in range(4):
        member = part_seq == float(seq)
        high = jnp.max(jnp.where(member, stats, LOW), axis=0, keepdims=True)
        factor = jnp.where(member, jnp.exp(stats - high), 0.0)
        sums = jnp.sum(factor * part_sum, axis=0, keepdims=True)
        for step in range(3):
            r = 3 * seq + step
            accs = jnp.sum(factor[:, step : step + 1] * zb2[:, step, :], axis=0, keepdims=True)
            x2send[r : r + 1, :] = accs
            x2send[16 + r : 17 + r, :] = jnp.where(
                lane1 < 64, high[:, step : step + 1], sums[:, step : step + 1]
            )
    x2buf[x] = x2send[...]
    for dx in range(1, XN):
        remote(
            x2send, x2buf.at[x], chain_send.at[5], chain_recv.at[5], {"ctx": at_x(dx)}
        ).start()
    bulk(5)
    wait_bytes(x2buf.at[pl.ds(0, XN - 1)], chain_recv.at[5])
    accs = x2buf[:, 0:16, :]
    stats = x2buf[:, 16:32, :]
    lane_x = lax.broadcasted_iota(jnp.int32, (4, 16, 128), 2)
    turned = swap_halves(stats, 2)
    part_high = jnp.where(lane_x < 64, stats, turned)
    part_sum = jnp.where(lane_x < 64, turned, stats)
    high = jnp.maximum(jnp.max(part_high, axis=0), fresh_high)
    factor = jnp.exp(part_high - high[None])
    fresh_weights = jnp.where(seen, jnp.exp(fresh - high[:, 0:1]), 0.0)
    sums = jnp.sum(factor * part_sum, axis=0) + jnp.sum(fresh_weights, axis=1, keepdims=True)
    mixed = jnp.sum(factor * accs, axis=0) + jnp.dot(
        fresh_weights.astype(jnp.bfloat16), new_values, preferred_element_type=jnp.float32
    )
    attention = (mixed / sums).astype(jnp.bfloat16)
    ats[...] = attention
    agb[head] = attention
    for dz in (1, -1, 2, -2, 3, -3, 4):
        remote(
            ats, agb.at[head], chain_send.at[6], chain_recv.at[6], {"ctx": at_z(dz + ZN)}
        ).start()
    bulk(6)
    cp_wo.wait()
    wait_bytes(agb.at[pl.ds(0, HEADS - 1)], chain_recv.at[6])

    out = jnp.zeros((16, 128), jnp.float32)
    for h in range(HEADS):
        out = out + jnp.dot(
            agb[h], wo[128 * h : 128 * h + 128, :], preferred_element_type=jnp.float32
        )
    osend[...] = out
    tbuf[mt] = out
    for dt in range(1, TP):
        remote(
            osend, tbuf.at[mt], chain_send.at[7], chain_recv.at[7], {"tp": (mt + dt) % TP}
        ).start()
    bulk(7)
    wait_bytes(tbuf.at[pl.ds(0, TP - 1)], chain_recv.at[7])
    out = jnp.sum(tbuf[...], axis=0)
    for step in range(3):
        for seq in range(4):
            r = 3 * seq + step
            fs[step, seq : seq + 1, :] = out[r : r + 1, :]
    att_ref[...] = fs[...].astype(jnp.bfloat16)

    wait_bytes(xbuf.at[pl.ds(0, XN - 1)], chain_send.at[0])
    wait_bytes(zbuf.at[pl.ds(0, ZN - 1)], chain_send.at[1])
    wait_bytes(gz.at[pl.ds(0, 7)], chain_send.at[2])
    wait_bytes(gbuf.at[pl.ds(0, XN - 1)], chain_send.at[3])
    wait_bytes(zb2.at[pl.ds(0, ZN - 1)], chain_send.at[4])
    wait_bytes(x2buf.at[pl.ds(0, XN - 1)], chain_send.at[5])
    wait_bytes(agb.at[pl.ds(0, HEADS - 1)], chain_send.at[6])
    wait_bytes(tbuf.at[pl.ds(0, TP - 1)], chain_send.at[7])
    cp_own.wait()
    others = pl.ds(0, 2 * (ZN * XN - 1))
    wait_bytes(packed.at[others], a2a_send)
    wait_bytes(rel_ref.at[others], a2a_recv)


PLAN = (((True, 0), ), ((False, 0), ), ((True, 1), ), ((False, 1), ), ((True, 2), (False, 2), ), (), ((True, 3), (False, 3), ), ())


def inverse_table():
    half = np.arange(64, dtype=np.float32)
    power = np.float32(-math.log(500000.0)) * half * np.float32(2.0) / np.float32(128.0)
    inverse = np.exp(power.astype(np.float64)).astype(np.float32)
    return np.concatenate([inverse, inverse])[None, :]


def body(
    new_hidden, norm_gain, qkv_weight, out_weight, owned_cache, lengths, owner_device, block_target
):
    f32, bf16, i32 = jnp.float32, jnp.bfloat16, jnp.int32
    vmem = pl.BlockSpec(memory_space=pltpu.VMEM)
    smem = pl.BlockSpec(memory_space=pltpu.SMEM)
    hbm = pl.BlockSpec(memory_space=pltpu.HBM)
    dma = pltpu.SemaphoreType.DMA
    attended, relaid = pl.pallas_call(
        kernel,
        out_shape=(
            jax.ShapeDtypeStruct((3, 4, 128), bf16),
            jax.ShapeDtypeStruct((128, 16, 256), bf16),
        ),
        in_specs=[smem] + [hbm] * 8,
        out_specs=(vmem, hbm),
        scratch_shapes=[
            pltpu.VMEM((3, 4, 128), bf16),
            pltpu.VMEM((1, 128), f32),
            pltpu.VMEM((1, 128), f32),
            pltpu.VMEM((1, 64), i32),
            pltpu.VMEM((1, 128), i32),
            pltpu.VMEM((64, 128), i32),
            pltpu.SMEM((64, 128), i32),
            pltpu.VMEM((128, 1280), bf16),
            pltpu.VMEM((1024, 128), bf16),
            pltpu.VMEM((128, 16, 256), bf16),
            pltpu.VMEM((128, 16, 256), bf16),
            pltpu.VMEM((16, 128), f32),
            pltpu.VMEM((128, 128), f32),
            pltpu.VMEM((4, 32, 128), f32),
            pltpu.VMEM((8, 4, 128), f32),
            pltpu.VMEM((16, 4, 128), f32),
            pltpu.VMEM((4, 128), f32),
            pltpu.VMEM((8, 4, 128), f32),
            pltpu.VMEM((32, 128), f32),
            pltpu.VMEM((4, 32, 128), f32),
            pltpu.VMEM((32, 128), f32),
            pltpu.VMEM((8, 4, 128), f32),
            pltpu.VMEM((16, 4, 128), f32),
            pltpu.VMEM((32, 128), f32),
            pltpu.VMEM((4, 32, 128), f32),
            pltpu.VMEM((16, 128), bf16),
            pltpu.VMEM((8, 16, 128), bf16),
            pltpu.VMEM((16, 128), f32),
            pltpu.VMEM((8, 16, 128), f32),
            pltpu.VMEM((3, 4, 128), f32),
            dma((9,)),
            dma,
            dma,
            dma,
            dma((8,)),
            dma((8,)),
        ],
        compiler_params=pltpu.CompilerParams(
            collective_id=0, has_side_effects=True, vmem_limit_bytes=VL * 1024 * 1024
        ),
        name="decode_and_relay",
    )(
        lengths,
        new_hidden,
        norm_gain.reshape(1, 128),
        jnp.asarray(inverse_table()),
        owner_device.reshape(1, 64),
        block_target.reshape(64, 1, 128),
        qkv_weight.reshape(128, 1280),
        out_weight.reshape(1024, 128),
        owned_cache.reshape(128, 16, 256),
    )
    return attended, relaid.reshape(128, 16, 1, 256)


def solution(mesh):
    in_specs = (
        P(None, None, "ctx"),
        P("ctx"),
        P("ctx", "tp", None),
        P("tp", None, "ctx"),
        P("ctx", None, "tp", None),
        P(),
        P(),
        P(),
    )
    out_specs = (P(None, None, "ctx"), P("ctx", None, "tp", None))
    return jax.shard_map(body, mesh=mesh, in_specs=in_specs, out_specs=out_specs, check_vma=False)
```

```python
import functools
import math

import jax
import jax.numpy as jnp
import numpy as np
from jax import lax
from jax.experimental import pallas as pl
from jax.experimental.pallas import tpu as pltpu
from jax.sharding import PartitionSpec as P

MESH = pl.DeviceIdType.MESH
ZN, XN, TP = 16, 4, 8
HEADS = 8
LOW = -1e30
VL = 60


def remote(src, dst, send, recv, target):
    return pltpu.make_async_remote_copy(
        src_ref=src,
        dst_ref=dst,
        send_sem=send,
        recv_sem=recv,
        device_id=target,
        device_id_type=MESH,
    )


def wait_bytes(ref, sem):
    pltpu.make_async_copy(ref, ref, sem).wait()


def swap_halves(values, axis):
    return pltpu.roll(values, 64, axis)


def kernel(
    len_ref, hid_hbm, gain_hbm, inv_hbm, own_hbm, tgt_hbm, wq_hbm, wo_hbm, cache_hbm,
    att_ref, rel_ref,
    hid_ref, gain_ref, inv_ref, own_ref, tgt, slot_v, slot_s, wq, wo, cache, packed,
    hid32, pbuf, xbuf, zsend, zbuf, asend, gbuf, kvs,
    bbuf, zb2, x2send, x2buf, ats, agb, osend, tbuf, fs,
    in_sem, own_sem, a2a_send, a2a_recv, chain_send, chain_recv,
):
    me = lax.axis_index("ctx")
    mt = lax.axis_index("tp")
    z = me // XN
    x = me % XN

    def at_z(dz):
        return ((z + dz) % ZN) * XN + x

    def at_x(dx):
        return z * XN + (x + dx) % XN

    barrier = pltpu.get_barrier_semaphore()

    def greet(offset):
        to = (me + ZN * XN + offset) % (ZN * XN)
        pl.semaphore_signal(barrier, inc=1, device_id={"ctx": to}, device_id_type=MESH)

    def greet_ctx(k, carry):
        greet(32 + k)
        greet(32 - k)
        return carry

    def greet_tp(k, carry):
        pl.semaphore_signal(barrier, inc=1, device_id={"tp": (mt + k) % TP}, device_id_type=MESH)
        return carry

    greet(32)
    lax.fori_loop(1, 32, greet_ctx, 0)
    lax.fori_loop(1, TP, greet_tp, 0)

    cp_tgt = pltpu.make_async_copy(tgt_hbm.at[me], tgt, in_sem.at[0])
    cp_wq = pltpu.make_async_copy(wq_hbm, wq, in_sem.at[1])
    cp_cache = pltpu.make_async_copy(cache_hbm, cache, in_sem.at[2])
    cp_wo = pltpu.make_async_copy(wo_hbm, wo, in_sem.at[3])
    cp_hid = pltpu.make_async_copy(hid_hbm, hid_ref, in_sem.at[5])
    cp_gain = pltpu.make_async_copy(gain_hbm, gain_ref, in_sem.at[6])
    cp_inv = pltpu.make_async_copy(inv_hbm, inv_ref, in_sem.at[7])
    cp_own_dev = pltpu.make_async_copy(own_hbm, own_ref, in_sem.at[8])
    cp_tgt.start()
    cp_hid.start()
    cp_gain.start()
    cp_wq.start()
    cp_cache.start()
    cp_inv.start()
    cp_own_dev.start()
    cp_wo.start()

    hid32[...] = jnp.zeros_like(hid32)
    cp_hid.wait()
    cp_gain.wait()
    for step in range(3):
        hid32[4 * step : 4 * step + 4, :] = hid_ref[step].astype(jnp.float32)
    hidden = hid32[...]
    scaled = (hidden * gain_ref[...]).astype(jnp.bfloat16)
    row16 = lax.broadcasted_iota(jnp.int32, (16, 128), 0)
    lane16 = lax.broadcasted_iota(jnp.int32, (16, 128), 1)
    squares = jnp.sum(hidden * hidden, axis=1, keepdims=True)
    square_row = jnp.sum(jnp.where(row16 == lane16, squares, 0.0), axis=0, keepdims=True)
    row8 = lax.broadcasted_iota(jnp.int32, (8, 128), 0)
    lane8 = lax.broadcasted_iota(jnp.int32, (8, 128), 1)
    pbuf[120:128, :] = jnp.where(row8 == 0, square_row, 0.0)
    cp_wq.wait()
    for head in range(HEADS + 2):
        part = jnp.dot(
            scaled, wq[:, 128 * head : 128 * head + 128], preferred_element_type=jnp.float32
        )
        pbuf[12 * head : 12 * head + 12, :] = part[0:12, :]

    cp_tgt.wait()
    t_iota = lax.broadcasted_iota(jnp.int32, (64, 128), 0)
    b_iota = lax.broadcasted_iota(jnp.int32, (64, 128), 1)
    match = tgt[...] == t_iota
    first = jnp.min(jnp.where(match, b_iota, 127), axis=1, keepdims=True)
    last = jnp.max(jnp.where(match, b_iota, 0), axis=1, keepdims=True)
    slot_v[...] = jnp.where(b_iota == 0, first, last)
    cp_slot = pltpu.make_async_copy(slot_v, slot_s, in_sem.at[4])
    cp_slot.start()
    cp_slot.wait()
    cp_cache.wait()

    def pack(t, carry):
        packed[2 * t] = cache[slot_s[t, 0]]
        packed[2 * t + 1] = cache[slot_s[t, 1]]
        return carry

    lax.fori_loop(0, ZN * XN, pack, 0)
    mine = pl.ds(2 * me, 2)
    cp_own = pltpu.make_async_copy(packed.at[mine], rel_ref.at[mine], own_sem)
    cp_own.start()

    row24 = lax.broadcasted_iota(jnp.int32, (24, 128), 0)
    lane24 = lax.broadcasted_iota(jnp.int32, (24, 128), 1)
    seq24 = row24 % 4
    row_in = row24 % 12
    length24 = jnp.where(
        seq24 == 0,
        len_ref[0],
        jnp.where(seq24 == 1, len_ref[1], jnp.where(seq24 == 2, len_ref[2], len_ref[3])),
    )
    position = length24.astype(jnp.float32) + (row_in // 4).astype(jnp.float32)
    cp_inv.wait()
    angle = position * inv_ref[...]
    cosine = jnp.cos(angle)
    sine = jnp.where(lane24 < 64, -jnp.sin(angle), jnp.sin(angle))

    cp_own_dev.wait()
    own_iota = lax.broadcasted_iota(jnp.int32, (1, 64), 1)
    segment = jnp.sum(jnp.where(own_ref[...] == me, own_iota, 0), axis=1, keepdims=True)
    my_seq = segment // 16
    my_offset = segment % 16 * 2048
    my_length = jnp.where(
        my_seq == 0,
        len_ref[0],
        jnp.where(my_seq == 1, len_ref[1], jnp.where(my_seq == 2, len_ref[2], len_ref[3])),
    )

    pl.semaphore_wait(barrier, ZN * XN - 1 + TP - 1)

    def send_blocks(dz, dx):
        to = ((z + dz + ZN) % ZN) * XN + (x + dx) % XN
        remote(
            packed.at[pl.ds(2 * to, 2)], rel_ref.at[mine], a2a_send, a2a_recv, {"ctx": to}
        ).start()

    def bulk(slot):
        for odd, dx in PLAN[slot]:

            def both_ways(step, carry):
                dz = 2 * step + 1 if odd else 2 * step
                send_blocks(dz, dx)
                send_blocks(-dz, dx)
                return carry

            if odd:
                lax.fori_loop(0, 4, both_ways, 0)
            else:
                send_blocks(8, dx)
                lax.fori_loop(1, 4, both_ways, 0)
                if dx > 0:
                    send_blocks(0, dx)

    def far_first(send):
        def both_ways(step, carry):
            send(ZN // 2 + step)
            send(ZN // 2 - step)
            return carry

        send(ZN // 2)
        lax.fori_loop(1, ZN // 2, both_ways, 0)

    quarter = pl.ds(pl.multiple_of(32 * x, 32), 32)
    for dx in (2, 1, 3):
        to = (x + dx) % XN
        remote(
            pbuf.at[pl.ds(pl.multiple_of(32 * to, 32), 32)], xbuf.at[x],
            chain_send.at[0], chain_recv.at[0], {"ctx": at_x(dx)},
        ).start()
    bulk(0)
    xbuf[x] = pbuf[quarter, :]
    wait_bytes(xbuf.at[pl.ds(0, XN - 1)], chain_recv.at[0])
    total = jnp.sum(xbuf[...], axis=0)
    zsend[...] = total.reshape(4, 8, 128)
    chunk = z % 4

    def scatter_a(dz):
        to = (z + dz) % ZN
        remote(
            zsend.at[to % 4], zbuf.at[z], chain_send.at[1], chain_recv.at[1], {"ctx": to * XN + x}
        ).start()

    far_first(scatter_a)
    bulk(1)
    zbuf[z] = zsend[chunk]
    wait_bytes(zbuf.at[pl.ds(0, ZN - 1)], chain_recv.at[1])
    total = jnp.sum(zbuf[...], axis=0)
    asend[...] = total
    gbuf[x, chunk] = total
    for dz, dx in ((2, 2), (2, 1), (2, 3), (1, 2), (-1, 2), (1, 1), (-1, 1), (1, 3), (-1, 3),
                   (2, 0), (0, 2), (1, 0), (-1, 0), (0, 1), (0, 3)):
        to = ((z + dz + ZN) % ZN) * XN + (x + dx) % XN
        remote(
            asend, gbuf.at[x, chunk], chain_send.at[2], chain_recv.at[2], {"ctx": to}
        ).start()
    bulk(2)
    wait_bytes(zbuf.at[pl.ds(0, 15)], chain_recv.at[2])

    whole = gbuf[...].reshape(128, 128)
    square_sum = jnp.sum(
        jnp.where(lane24 == row_in, whole[120:121, :], 0.0), axis=1, keepdims=True
    )
    norm = jnp.sqrt(square_sum / 8192.0 + 1e-05)
    rotated = []
    for g in range(5):
        plain = whole[24 * g : 24 * g + 24, :] / norm
        turned = plain * cosine + swap_halves(plain, 1) * sine
        if g < 4:
            rotated.append(turned)
        else:
            kvs[0:24, :] = jnp.where(row24 < 12, turned, plain)
    kvs[24:32, :] = jnp.zeros((8, 128), jnp.float32)
    queries = jnp.concatenate(rotated, axis=0).astype(jnp.bfloat16)

    pick_row = lax.broadcasted_iota(jnp.int32, (32, 96), 0)
    pick_col = lax.broadcasted_iota(jnp.int32, (32, 96), 1)
    wanted = 12 * (pick_row // 4) + 4 * (pick_row % 4) + my_seq
    pick = jnp.where((wanted == pick_col) & (pick_row % 4 < 3), 1.0, 0.0).astype(jnp.bfloat16)
    my_queries = jnp.dot(pick, queries, preferred_element_type=jnp.float32).astype(jnp.bfloat16)
    keys = cache[:, :, 0:128].reshape(2048, 128)
    values = cache[:, :, 128:256].reshape(2048, 128)
    scale = 1.0 / math.sqrt(128)
    scores = (
        lax.dot_general(
            my_queries, keys, (((1,), (1,)), ((), ())), preferred_element_type=jnp.float32
        )
        * scale
    )
    place = my_offset + lax.broadcasted_iota(jnp.int32, (1, 2048), 1)
    live = place < my_length
    scores = jnp.where(live, scores, LOW)
    highest = jnp.max(scores, axis=1, keepdims=True)
    weights = jnp.where(live, jnp.exp(scores - highest), 0.0)
    weight_sum = jnp.sum(weights, axis=1, keepdims=True)
    weighted = jnp.dot(weights.astype(jnp.bfloat16), values, preferred_element_type=jnp.float32)
    row32 = lax.broadcasted_iota(jnp.int32, (32, 128), 0) % 4
    lane32 = lax.broadcasted_iota(jnp.int32, (32, 128), 1)
    stats = jnp.where(lane32 < 3, highest, weight_sum)
    placed = my_seq.astype(jnp.float32)
    for step in range(3):
        shifted = pltpu.roll(stats, 3 - step, 0)
        placed = jnp.where((lane32 == step) | (lane32 == 3 + step), shifted, placed)
    partial = jnp.where(row32 < 3, weighted, placed)
    for h in range(HEADS):
        bbuf[h] = partial[4 * h : 4 * h + 4, :]

    head = z % HEADS

    def scatter_b(dz):
        to = (z + dz) % ZN
        remote(
            bbuf.at[to % HEADS], zb2.at[z], chain_send.at[3], chain_recv.at[3], {"ctx": to * XN + x}
        ).start()

    far_first(scatter_b)
    bulk(3)
    zb2[z] = bbuf[head]

    pick_row = lax.broadcasted_iota(jnp.int32, (16, 96), 0)
    pick_col = lax.broadcasted_iota(jnp.int32, (16, 96), 1)
    wanted = 12 * head + 4 * (pick_row % 3) + pick_row // 3
    pick = jnp.where((wanted == pick_col) & (pick_row < 12), 1.0, 0.0).astype(jnp.bfloat16)
    head_queries = jnp.dot(pick, queries, preferred_element_type=jnp.float32).astype(jnp.bfloat16)
    new_keys = kvs[0:16, :].astype(jnp.bfloat16)
    new_values = kvs[12:28, :].astype(jnp.bfloat16)
    fresh = (
        lax.dot_general(
            head_queries, new_keys, (((1,), (1,)), ((), ())), preferred_element_type=jnp.float32
        )
        * scale
    )
    q_row = lax.broadcasted_iota(jnp.int32, (16, 16), 0)
    k_col = lax.broadcasted_iota(jnp.int32, (16, 16), 1)
    seen = (
        (q_row // 3 == k_col % 4) & (k_col // 4 <= q_row % 3) & (k_col < 12) & (q_row < 12)
    )
    fresh = jnp.where(seen, fresh, LOW)
    fresh_high = jnp.max(fresh, axis=1, keepdims=True)
    x2send[...] = jnp.where(lax.broadcasted_iota(jnp.int32, (32, 128), 0) < 16, 0.0, 1.0)

    wait_bytes(zb2.at[pl.ds(0, ZN - 1)], chain_recv.at[3])
    stats = zb2[:, 3, :]
    part_sum = pltpu.roll(stats, 125, 1)
    part_seq = stats[:, 6:7]
    lane1 = lax.broadcasted_iota(jnp.int32, (1, 128), 1)
    for seq in range(4):
        member = part_seq == float(seq)
        high = jnp.max(jnp.where(member, stats, LOW), axis=0, keepdims=True)
        factor = jnp.where(member, jnp.exp(stats - high), 0.0)
        sums = jnp.sum(factor * part_sum, axis=0, keepdims=True)
        for step in range(3):
            r = 3 * seq + step
            accs = jnp.sum(factor[:, step : step + 1] * zb2[:, step, :], axis=0, keepdims=True)
            x2send[r : r + 1, :] = accs
            x2send[16 + r : 17 + r, :] = jnp.where(
                lane1 < 64, high[:, step : step + 1], sums[:, step : step + 1]
            )
    x2buf[x] = x2send[...]
    for dx in (2, 1, 3):
        remote(
            x2send, x2buf.at[x], chain_send.at[4], chain_recv.at[4], {"ctx": at_x(dx)}
        ).start()
    bulk(4)
    wait_bytes(x2buf.at[pl.ds(0, XN - 1)], chain_recv.at[4])
    accs = x2buf[:, 0:16, :]
    stats = x2buf[:, 16:32, :]
    lane_x = lax.broadcasted_iota(jnp.int32, (4, 16, 128), 2)
    turned = swap_halves(stats, 2)
    part_high = jnp.where(lane_x < 64, stats, turned)
    part_sum = jnp.where(lane_x < 64, turned, stats)
    high = jnp.maximum(jnp.max(part_high, axis=0), fresh_high)
    factor = jnp.exp(part_high - high[None])
    fresh_weights = jnp.where(seen, jnp.exp(fresh - high[:, 0:1]), 0.0)
    sums = jnp.sum(factor * part_sum, axis=0) + jnp.sum(fresh_weights, axis=1, keepdims=True)
    mixed = jnp.sum(factor * accs, axis=0) + jnp.dot(
        fresh_weights.astype(jnp.bfloat16), new_values, preferred_element_type=jnp.float32
    )
    attention = (mixed / sums).astype(jnp.bfloat16)
    ats[...] = attention
    agb[head] = attention
    for dz in (4, 3, -3, 2, -2, 1, -1):
        remote(
            ats, agb.at[head], chain_send.at[5], chain_recv.at[5], {"ctx": at_z(dz + ZN)}
        ).start()
    bulk(5)
    cp_wo.wait()
    wait_bytes(agb.at[pl.ds(0, HEADS - 1)], chain_recv.at[5])

    out = jnp.zeros((16, 128), jnp.float32)
    for h in range(HEADS):
        out = out + jnp.dot(
            agb[h], wo[128 * h : 128 * h + 128, :], preferred_element_type=jnp.float32
        )
    osend[...] = out
    tbuf[mt] = out
    for dt in (4, 5, 3, 2, 6, 1, 7):
        remote(
            osend, tbuf.at[mt], chain_send.at[6], chain_recv.at[6], {"tp": (mt + dt) % TP}
        ).start()
    bulk(6)
    wait_bytes(tbuf.at[pl.ds(0, TP - 1)], chain_recv.at[6])
    out = jnp.sum(tbuf[...], axis=0)
    for step in range(3):
        for seq in range(4):
            r = 3 * seq + step
            fs[step, seq : seq + 1, :] = out[r : r + 1, :]
    att_ref[...] = fs[...].astype(jnp.bfloat16)

    wait_bytes(xbuf.at[pl.ds(0, XN - 1)], chain_send.at[0])
    wait_bytes(zbuf.at[pl.ds(0, ZN - 1)], chain_send.at[1])
    wait_bytes(zbuf.at[pl.ds(0, 15)], chain_send.at[2])
    wait_bytes(zb2.at[pl.ds(0, ZN - 1)], chain_send.at[3])
    wait_bytes(x2buf.at[pl.ds(0, XN - 1)], chain_send.at[4])
    wait_bytes(agb.at[pl.ds(0, HEADS - 1)], chain_send.at[5])
    wait_bytes(tbuf.at[pl.ds(0, TP - 1)], chain_send.at[6])
    cp_own.wait()
    others = pl.ds(0, 2 * (ZN * XN - 1))
    wait_bytes(packed.at[others], a2a_send)
    wait_bytes(rel_ref.at[others], a2a_recv)


PLAN = (((True, 0), ), ((False, 0), ), ((True, 1), ), ((False, 1), (True, 2), ), ((False, 2), ), ((True, 3), (False, 3), ), ())


def inverse_table():
    half = np.arange(64, dtype=np.float32)
    power = np.float32(-math.log(500000.0)) * half * np.float32(2.0) / np.float32(128.0)
    inverse = np.exp(power.astype(np.float64)).astype(np.float32)
    return np.concatenate([inverse, inverse])[None, :]


def body(
    new_hidden, norm_gain, qkv_weight, out_weight, owned_cache, lengths, owner_device, block_target
):
    f32, bf16, i32 = jnp.float32, jnp.bfloat16, jnp.int32
    vmem = pl.BlockSpec(memory_space=pltpu.VMEM)
    smem = pl.BlockSpec(memory_space=pltpu.SMEM)
    hbm = pl.BlockSpec(memory_space=pltpu.HBM)
    dma = pltpu.SemaphoreType.DMA
    attended, relaid = pl.pallas_call(
        kernel,
        out_shape=(
            pltpu.VMEM((3, 4, 128), bf16),
            pltpu.VMEM((128, 16, 256), bf16),
        ),
        in_specs=[smem] + [hbm] * 8,
        out_specs=(vmem, vmem),
        scratch_shapes=[
            pltpu.VMEM((3, 4, 128), bf16),
            pltpu.VMEM((1, 128), f32),
            pltpu.VMEM((1, 128), f32),
            pltpu.VMEM((1, 64), i32),
            pltpu.VMEM((1, 128), i32),
            pltpu.VMEM((64, 128), i32),
            pltpu.SMEM((64, 128), i32),
            pltpu.VMEM((128, 1280), bf16),
            pltpu.VMEM((1024, 128), bf16),
            pltpu.VMEM((128, 16, 256), bf16),
            pltpu.VMEM((128, 16, 256), bf16),
            pltpu.VMEM((16, 128), f32),
            pltpu.VMEM((128, 128), f32),
            pltpu.VMEM((4, 32, 128), f32),
            pltpu.VMEM((4, 8, 128), f32),
            pltpu.VMEM((16, 8, 128), f32),
            pltpu.VMEM((8, 128), f32),
            pltpu.VMEM((4, 4, 8, 128), f32),
            pltpu.VMEM((32, 128), f32),
            pltpu.VMEM((8, 4, 128), f32),
            pltpu.VMEM((16, 4, 128), f32),
            pltpu.VMEM((32, 128), f32),
            pltpu.VMEM((4, 32, 128), f32),
            pltpu.VMEM((16, 128), bf16),
            pltpu.VMEM((8, 16, 128), bf16),
            pltpu.VMEM((16, 128), f32),
            pltpu.VMEM((8, 16, 128), f32),
            pltpu.VMEM((3, 4, 128), f32),
            dma((9,)),
            dma,
            dma,
            dma,
            dma((7,)),
            dma((7,)),
        ],
        compiler_params=pltpu.CompilerParams(
            collective_id=0, has_side_effects=True, vmem_limit_bytes=VL * 1024 * 1024
        ),
        name="decode_and_relay",
    )(
        lengths,
        new_hidden,
        norm_gain.reshape(1, 128),
        jnp.asarray(inverse_table()),
        owner_device.reshape(1, 64),
        block_target.reshape(64, 1, 128),
        qkv_weight.reshape(128, 1280),
        out_weight.reshape(1024, 128),
        owned_cache.reshape(128, 16, 256),
    )
    return attended, relaid.reshape(128, 16, 1, 256)


def solution(mesh):
    in_specs = (
        P(None, None, "ctx"),
        P("ctx"),
        P("ctx", "tp", None),
        P("tp", None, "ctx"),
        P("ctx", None, "tp", None),
        P(),
        P(),
        P(),
    )
    out_specs = (P(None, None, "ctx"), P("ctx", None, "tp", None))
    return jax.shard_map(body, mesh=mesh, in_specs=in_specs, out_specs=out_specs, check_vma=False)
```

```python
import functools
import math

import jax
import jax.numpy as jnp
import numpy as np
from jax import lax
from jax.experimental import pallas as pl
from jax.experimental.pallas import tpu as pltpu
from jax.sharding import PartitionSpec as P

MESH = pl.DeviceIdType.MESH
ZN, XN, TP = 16, 4, 8
HEADS = 8
LOW = -1e30
VL = 60


def remote(src, dst, send, recv, target):
    return pltpu.make_async_remote_copy(
        src_ref=src,
        dst_ref=dst,
        send_sem=send,
        recv_sem=recv,
        device_id=target,
        device_id_type=MESH,
    )


def wait_bytes(ref, sem):
    pltpu.make_async_copy(ref, ref, sem).wait()


def swap_halves(values, axis):
    return pltpu.roll(values, 64, axis)


def kernel(
    len_ref, hid_hbm, gain_hbm, inv_hbm, own_hbm, tgt_hbm, wq_hbm, wo_hbm, cache_hbm,
    att_ref, rel_ref,
    hid_ref, gain_ref, inv_ref, own_ref, tgt, slot_v, slot_s, wq, wo, cache, packed,
    hid32, pbuf, xbuf, zsend, zbuf, asend, gbuf, kvs,
    bbuf, zb2, x2send, x2buf, ats, agb, osend, tbuf, fs,
    in_sem, own_sem, a2a_send, a2a_recv, chain_send, chain_recv, ready,
):
    me = lax.axis_index("ctx")
    mt = lax.axis_index("tp")
    z = me // XN
    x = me % XN

    def at_z(dz):
        return ((z + dz) % ZN) * XN + x

    def at_x(dx):
        return z * XN + (x + dx) % XN

    barrier = pltpu.get_barrier_semaphore()

    def greet(dz, dx):
        to = ((z + dz + ZN) % ZN) * XN + (x + dx) % XN
        pl.semaphore_signal(barrier, inc=1, device_id={"ctx": to}, device_id_type=MESH)

    def greet_both(step, carry):
        for dx in range(XN):
            greet(4 - step, dx)
            greet(step - 4, dx)
        return carry

    def greet_tp(k, carry):
        pl.semaphore_signal(barrier, inc=1, device_id={"tp": (mt + k) % TP}, device_id_type=MESH)
        return carry

    lax.fori_loop(0, 4, greet_both, 0)
    for dx in range(1, XN):
        greet(0, dx)
    lax.fori_loop(1, TP, greet_tp, 0)

    cp_tgt = pltpu.make_async_copy(tgt_hbm.at[me], tgt, in_sem.at[0])
    cp_wq = pltpu.make_async_copy(wq_hbm, wq, in_sem.at[1])
    cp_cache = pltpu.make_async_copy(cache_hbm, cache, in_sem.at[2])
    cp_wo = pltpu.make_async_copy(wo_hbm, wo, in_sem.at[3])
    cp_hid = pltpu.make_async_copy(hid_hbm, hid_ref, in_sem.at[5])
    cp_gain = pltpu.make_async_copy(gain_hbm, gain_ref, in_sem.at[6])
    cp_inv = pltpu.make_async_copy(inv_hbm, inv_ref, in_sem.at[7])
    cp_own_dev = pltpu.make_async_copy(own_hbm, own_ref, in_sem.at[8])
    cp_tgt.start()
    cp_hid.start()
    cp_gain.start()
    cp_wq.start()
    cp_cache.start()
    cp_inv.start()
    cp_own_dev.start()
    cp_wo.start()

    hid32[...] = jnp.zeros_like(hid32)
    cp_hid.wait()
    cp_gain.wait()
    for step in range(3):
        hid32[4 * step : 4 * step + 4, :] = hid_ref[step].astype(jnp.float32)
    hidden = hid32[...]
    scaled = (hidden * gain_ref[...]).astype(jnp.bfloat16)
    row16 = lax.broadcasted_iota(jnp.int32, (16, 128), 0)
    lane16 = lax.broadcasted_iota(jnp.int32, (16, 128), 1)
    squares = jnp.sum(hidden * hidden, axis=1, keepdims=True)
    square_row = jnp.sum(jnp.where(row16 == lane16, squares, 0.0), axis=0, keepdims=True)
    row8 = lax.broadcasted_iota(jnp.int32, (8, 128), 0)
    lane8 = lax.broadcasted_iota(jnp.int32, (8, 128), 1)
    pbuf[120:128, :] = jnp.where(row8 == 0, square_row, 0.0)
    cp_wq.wait()
    for head in range(HEADS + 2):
        part = jnp.dot(
            scaled, wq[:, 128 * head : 128 * head + 128], preferred_element_type=jnp.float32
        )
        pbuf[12 * head : 12 * head + 12, :] = part[0:12, :]

    cp_tgt.wait()
    t_iota = lax.broadcasted_iota(jnp.int32, (64, 128), 0)
    b_iota = lax.broadcasted_iota(jnp.int32, (64, 128), 1)
    match = tgt[...] == t_iota
    first = jnp.min(jnp.where(match, b_iota, 127), axis=1, keepdims=True)
    last = jnp.max(jnp.where(match, b_iota, 0), axis=1, keepdims=True)
    slot_v[...] = jnp.where(b_iota == 0, first, last)
    cp_slot = pltpu.make_async_copy(slot_v, slot_s, in_sem.at[4])
    cp_slot.start()
    def send_blocks(dz, dx):
        to = ((z + dz + ZN) % ZN) * XN + (x + dx) % XN
        remote(
            packed.at[pl.ds(2 * to, 2)], rel_ref.at[mine], a2a_send, a2a_recv, {"ctx": to}
        ).start()

    def bulk(slot):
        for shifts, low, high in PLAN[slot]:

            def one(dx, carry):
                for dz in shifts:
                    send_blocks(dz, dx)
                return carry

            lax.fori_loop(low, high, one, 0)

    def far_first(send):
        def both_ways(step, carry):
            send(ZN // 2 + step)
            send(ZN // 2 - step)
            return carry

        send(ZN // 2)
        lax.fori_loop(1, ZN // 2, both_ways, 0)

    pl.semaphore_wait(barrier, 9 * XN - 1 + TP - 1)
    for dz in (4, -4):
        pl.semaphore_signal(ready, inc=1, device_id={"ctx": at_z(dz + ZN)}, device_id_type=MESH)

    quarter = pl.ds(pl.multiple_of(32 * x, 32), 32)
    for dx in (2, 1, 3):
        to = (x + dx) % XN
        remote(
            pbuf.at[pl.ds(pl.multiple_of(32 * to, 32), 32)], xbuf.at[x],
            chain_send.at[0], chain_recv.at[0], {"ctx": at_x(dx)},
        ).start()

    cp_slot.wait()
    cp_cache.wait()

    def pack(t, carry):
        packed[2 * t] = cache[slot_s[t, 0]]
        packed[2 * t + 1] = cache[slot_s[t, 1]]
        return carry

    lax.fori_loop(0, ZN * XN, pack, 0)
    mine = pl.ds(2 * me, 2)
    cp_own = pltpu.make_async_copy(packed.at[mine], rel_ref.at[mine], own_sem)
    cp_own.start()

    bulk(0)
    xbuf[x] = pbuf[quarter, :]
    wait_bytes(xbuf.at[pl.ds(0, XN - 1)], chain_recv.at[0])
    total = jnp.sum(xbuf[...], axis=0)
    pl.semaphore_wait(ready, 2)
    zsend[...] = total.reshape(4, 8, 128)
    chunk = z % 4

    def scatter_a(dz):
        to = (z + dz) % ZN
        remote(
            zsend.at[to % 4], zbuf.at[z], chain_send.at[1], chain_recv.at[1], {"ctx": to * XN + x}
        ).start()

    far_first(scatter_a)
    bulk(1)

    row24 = lax.broadcasted_iota(jnp.int32, (24, 128), 0)
    lane24 = lax.broadcasted_iota(jnp.int32, (24, 128), 1)
    seq24 = row24 % 4
    row_in = row24 % 12
    length24 = jnp.where(
        seq24 == 0,
        len_ref[0],
        jnp.where(seq24 == 1, len_ref[1], jnp.where(seq24 == 2, len_ref[2], len_ref[3])),
    )
    position = length24.astype(jnp.float32) + (row_in // 4).astype(jnp.float32)
    cp_inv.wait()
    angle = position * inv_ref[...]
    cosine = jnp.cos(angle)
    sine = jnp.where(lane24 < 64, -jnp.sin(angle), jnp.sin(angle))

    cp_own_dev.wait()
    own_iota = lax.broadcasted_iota(jnp.int32, (1, 64), 1)
    segment = jnp.sum(jnp.where(own_ref[...] == me, own_iota, 0), axis=1, keepdims=True)
    my_seq = segment // 16
    my_offset = segment % 16 * 2048
    my_length = jnp.where(
        my_seq == 0,
        len_ref[0],
        jnp.where(my_seq == 1, len_ref[1], jnp.where(my_seq == 2, len_ref[2], len_ref[3])),
    )

    zbuf[z] = zsend[chunk]
    wait_bytes(zbuf.at[pl.ds(0, ZN - 1)], chain_recv.at[1])
    total = jnp.sum(zbuf[...], axis=0)
    asend[...] = total
    gbuf[x, chunk] = total
    for dz, dx in ((2, 2), (2, 1), (2, 3), (1, 2), (-1, 2), (1, 1), (-1, 1), (1, 3), (-1, 3),
                   (2, 0), (0, 2), (1, 0), (-1, 0), (0, 1), (0, 3)):
        to = ((z + dz + ZN) % ZN) * XN + (x + dx) % XN
        remote(
            asend, gbuf.at[x, chunk], chain_send.at[2], chain_recv.at[2], {"ctx": to}
        ).start()
    bulk(2)
    wait_bytes(zbuf.at[pl.ds(0, 15)], chain_recv.at[2])

    whole = gbuf[...].reshape(128, 128)
    square_sum = jnp.sum(
        jnp.where(lane24 == row_in, whole[120:121, :], 0.0), axis=1, keepdims=True
    )
    norm = jnp.sqrt(square_sum / 8192.0 + 1e-05)
    rotated = []
    for g in range(5):
        plain = whole[24 * g : 24 * g + 24, :] / norm
        turned = plain * cosine + swap_halves(plain, 1) * sine
        if g < 4:
            rotated.append(turned)
        else:
            kvs[0:24, :] = jnp.where(row24 < 12, turned, plain)
    kvs[24:32, :] = jnp.zeros((8, 128), jnp.float32)
    queries = jnp.concatenate(rotated, axis=0).astype(jnp.bfloat16)

    pick_row = lax.broadcasted_iota(jnp.int32, (32, 96), 0)
    pick_col = lax.broadcasted_iota(jnp.int32, (32, 96), 1)
    wanted = 12 * (pick_row // 4) + 4 * (pick_row % 4) + my_seq
    pick = jnp.where((wanted == pick_col) & (pick_row % 4 < 3), 1.0, 0.0).astype(jnp.bfloat16)
    my_queries = jnp.dot(pick, queries, preferred_element_type=jnp.float32).astype(jnp.bfloat16)
    keys = cache[:, :, 0:128].reshape(2048, 128)
    values = cache[:, :, 128:256].reshape(2048, 128)
    scale = 1.0 / math.sqrt(128)
    scores = (
        lax.dot_general(
            my_queries, keys, (((1,), (1,)), ((), ())), preferred_element_type=jnp.float32
        )
        * scale
    )
    place = my_offset + lax.broadcasted_iota(jnp.int32, (1, 2048), 1)
    live = place < my_length
    scores = jnp.where(live, scores, LOW)
    highest = jnp.max(scores, axis=1, keepdims=True)
    weights = jnp.where(live, jnp.exp(scores - highest), 0.0)
    weight_sum = jnp.sum(weights, axis=1, keepdims=True)
    weighted = jnp.dot(weights.astype(jnp.bfloat16), values, preferred_element_type=jnp.float32)
    row32 = lax.broadcasted_iota(jnp.int32, (32, 128), 0) % 4
    lane32 = lax.broadcasted_iota(jnp.int32, (32, 128), 1)
    stats = jnp.where(lane32 < 3, highest, weight_sum)
    placed = my_seq.astype(jnp.float32)
    for step in range(3):
        shifted = pltpu.roll(stats, 3 - step, 0)
        placed = jnp.where((lane32 == step) | (lane32 == 3 + step), shifted, placed)
    partial = jnp.where(row32 < 3, weighted, placed)
    for h in range(HEADS):
        bbuf[h] = partial[4 * h : 4 * h + 4, :]

    head = z % HEADS

    def scatter_b(dz):
        to = (z + dz) % ZN
        remote(
            bbuf.at[to % HEADS], zb2.at[z], chain_send.at[3], chain_recv.at[3], {"ctx": to * XN + x}
        ).start()

    far_first(scatter_b)
    bulk(3)
    zb2[z] = bbuf[head]

    pick_row = lax.broadcasted_iota(jnp.int32, (16, 96), 0)
    pick_col = lax.broadcasted_iota(jnp.int32, (16, 96), 1)
    wanted = 12 * head + 4 * (pick_row % 3) + pick_row // 3
    pick = jnp.where((wanted == pick_col) & (pick_row < 12), 1.0, 0.0).astype(jnp.bfloat16)
    head_queries = jnp.dot(pick, queries, preferred_element_type=jnp.float32).astype(jnp.bfloat16)
    new_keys = kvs[0:16, :].astype(jnp.bfloat16)
    new_values = kvs[12:28, :].astype(jnp.bfloat16)
    fresh = (
        lax.dot_general(
            head_queries, new_keys, (((1,), (1,)), ((), ())), preferred_element_type=jnp.float32
        )
        * scale
    )
    q_row = lax.broadcasted_iota(jnp.int32, (16, 16), 0)
    k_col = lax.broadcasted_iota(jnp.int32, (16, 16), 1)
    seen = (
        (q_row // 3 == k_col % 4) & (k_col // 4 <= q_row % 3) & (k_col < 12) & (q_row < 12)
    )
    fresh = jnp.where(seen, fresh, LOW)
    fresh_high = jnp.max(fresh, axis=1, keepdims=True)
    x2send[...] = jnp.where(lax.broadcasted_iota(jnp.int32, (32, 128), 0) < 16, 0.0, 1.0)

    wait_bytes(zb2.at[pl.ds(0, ZN - 1)], chain_recv.at[3])
    stats = zb2[:, 3, :]
    part_sum = pltpu.roll(stats, 125, 1)
    part_seq = stats[:, 6:7]
    lane1 = lax.broadcasted_iota(jnp.int32, (1, 128), 1)
    for seq in range(4):
        member = part_seq == float(seq)
        high = jnp.max(jnp.where(member, stats, LOW), axis=0, keepdims=True)
        factor = jnp.where(member, jnp.exp(stats - high), 0.0)
        sums = jnp.sum(factor * part_sum, axis=0, keepdims=True)
        for step in range(3):
            r = 3 * seq + step
            accs = jnp.sum(factor[:, step : step + 1] * zb2[:, step, :], axis=0, keepdims=True)
            x2send[r : r + 1, :] = accs
            x2send[16 + r : 17 + r, :] = jnp.where(
                lane1 < 64, high[:, step : step + 1], sums[:, step : step + 1]
            )
    x2buf[x] = x2send[...]
    for dx in (2, 1, 3):
        remote(
            x2send, x2buf.at[x], chain_send.at[4], chain_recv.at[4], {"ctx": at_x(dx)}
        ).start()
    bulk(4)
    wait_bytes(x2buf.at[pl.ds(0, XN - 1)], chain_recv.at[4])
    accs = x2buf[:, 0:16, :]
    stats = x2buf[:, 16:32, :]
    lane_x = lax.broadcasted_iota(jnp.int32, (4, 16, 128), 2)
    turned = swap_halves(stats, 2)
    part_high = jnp.where(lane_x < 64, stats, turned)
    part_sum = jnp.where(lane_x < 64, turned, stats)
    high = jnp.maximum(jnp.max(part_high, axis=0), fresh_high)
    factor = jnp.exp(part_high - high[None])
    fresh_weights = jnp.where(seen, jnp.exp(fresh - high[:, 0:1]), 0.0)
    sums = jnp.sum(factor * part_sum, axis=0) + jnp.sum(fresh_weights, axis=1, keepdims=True)
    mixed = jnp.sum(factor * accs, axis=0) + jnp.dot(
        fresh_weights.astype(jnp.bfloat16), new_values, preferred_element_type=jnp.float32
    )
    attention = (mixed / sums).astype(jnp.bfloat16)
    ats[...] = attention
    agb[head] = attention
    for dz in (4, 3, -3, 2, -2, 1, -1):
        remote(
            ats, agb.at[head], chain_send.at[5], chain_recv.at[5], {"ctx": at_z(dz + ZN)}
        ).start()
    bulk(5)
    cp_wo.wait()
    wait_bytes(agb.at[pl.ds(0, HEADS - 1)], chain_recv.at[5])

    out = jnp.zeros((16, 128), jnp.float32)
    for h in range(HEADS):
        out = out + jnp.dot(
            agb[h], wo[128 * h : 128 * h + 128, :], preferred_element_type=jnp.float32
        )
    osend[...] = out
    tbuf[mt] = out
    for dt in (4, 5, 3, 2, 6, 1, 7):
        remote(
            osend, tbuf.at[mt], chain_send.at[6], chain_recv.at[6], {"tp": (mt + dt) % TP}
        ).start()
    bulk(6)
    wait_bytes(tbuf.at[pl.ds(0, TP - 1)], chain_recv.at[6])
    out = jnp.sum(tbuf[...], axis=0)
    for step in range(3):
        for seq in range(4):
            r = 3 * seq + step
            fs[step, seq : seq + 1, :] = out[r : r + 1, :]
    att_ref[...] = fs[...].astype(jnp.bfloat16)

    wait_bytes(xbuf.at[pl.ds(0, XN - 1)], chain_send.at[0])
    wait_bytes(zbuf.at[pl.ds(0, ZN - 1)], chain_send.at[1])
    wait_bytes(zbuf.at[pl.ds(0, 15)], chain_send.at[2])
    wait_bytes(zb2.at[pl.ds(0, ZN - 1)], chain_send.at[3])
    wait_bytes(x2buf.at[pl.ds(0, XN - 1)], chain_send.at[4])
    wait_bytes(agb.at[pl.ds(0, HEADS - 1)], chain_send.at[5])
    wait_bytes(tbuf.at[pl.ds(0, TP - 1)], chain_send.at[6])
    cp_own.wait()
    others = pl.ds(0, 2 * (ZN * XN - 1))
    wait_bytes(packed.at[others], a2a_send)
    wait_bytes(rel_ref.at[others], a2a_recv)


NEAR = (((1, -1, 2, -2), 0, 4), ((0,), 1, 4))
PLAN = (NEAR, (((8,), 0, 4), ((7, -7), 0, 2)), (((7, -7), 2, 4),), (((6, -6), 0, 4), ((5, -5), 0, 2)), (), (((5, -5), 2, 4), ((4, -4), 0, 4)), (((3, -3), 0, 4),))


def inverse_table():
    half = np.arange(64, dtype=np.float32)
    power = np.float32(-math.log(500000.0)) * half * np.float32(2.0) / np.float32(128.0)
    inverse = np.exp(power.astype(np.float64)).astype(np.float32)
    return np.concatenate([inverse, inverse])[None, :]


def body(
    new_hidden, norm_gain, qkv_weight, out_weight, owned_cache, lengths, owner_device, block_target
):
    f32, bf16, i32 = jnp.float32, jnp.bfloat16, jnp.int32
    vmem = pl.BlockSpec(memory_space=pltpu.VMEM)
    smem = pl.BlockSpec(memory_space=pltpu.SMEM)
    hbm = pl.BlockSpec(memory_space=pltpu.HBM)
    dma = pltpu.SemaphoreType.DMA
    attended, relaid = pl.pallas_call(
        kernel,
        out_shape=(
            pltpu.VMEM((3, 4, 128), bf16),
            pltpu.VMEM((128, 16, 256), bf16),
        ),
        in_specs=[smem] + [hbm] * 8,
        out_specs=(vmem, vmem),
        scratch_shapes=[
            pltpu.VMEM((3, 4, 128), bf16),
            pltpu.VMEM((1, 128), f32),
            pltpu.VMEM((1, 128), f32),
            pltpu.VMEM((1, 64), i32),
            pltpu.VMEM((1, 128), i32),
            pltpu.VMEM((64, 128), i32),
            pltpu.SMEM((64, 128), i32),
            pltpu.VMEM((128, 1280), bf16),
            pltpu.VMEM((1024, 128), bf16),
            pltpu.VMEM((128, 16, 256), bf16),
            pltpu.VMEM((128, 16, 256), bf16),
            pltpu.VMEM((16, 128), f32),
            pltpu.VMEM((128, 128), f32),
            pltpu.VMEM((4, 32, 128), f32),
            pltpu.VMEM((4, 8, 128), f32),
            pltpu.VMEM((16, 8, 128), f32),
            pltpu.VMEM((8, 128), f32),
            pltpu.VMEM((4, 4, 8, 128), f32),
            pltpu.VMEM((32, 128), f32),
            pltpu.VMEM((8, 4, 128), f32),
            pltpu.VMEM((16, 4, 128), f32),
            pltpu.VMEM((32, 128), f32),
            pltpu.VMEM((4, 32, 128), f32),
            pltpu.VMEM((16, 128), bf16),
            pltpu.VMEM((8, 16, 128), bf16),
            pltpu.VMEM((16, 128), f32),
            pltpu.VMEM((8, 16, 128), f32),
            pltpu.VMEM((3, 4, 128), f32),
            dma((9,)),
            dma,
            dma,
            dma,
            dma((7,)),
            dma((7,)),
            pltpu.SemaphoreType.REGULAR,
        ],
        compiler_params=pltpu.CompilerParams(
            collective_id=0, has_side_effects=True, vmem_limit_bytes=VL * 1024 * 1024
        ),
        name="decode_and_relay",
    )(
        lengths,
        new_hidden,
        norm_gain.reshape(1, 128),
        jnp.asarray(inverse_table()),
        owner_device.reshape(1, 64),
        block_target.reshape(64, 1, 128),
        qkv_weight.reshape(128, 1280),
        out_weight.reshape(1024, 128),
        owned_cache.reshape(128, 16, 256),
    )
    return attended, relaid.reshape(128, 16, 1, 256)


def solution(mesh):
    in_specs = (
        P(None, None, "ctx"),
        P("ctx"),
        P("ctx", "tp", None),
        P("tp", None, "ctx"),
        P("ctx", None, "tp", None),
        P(),
        P(),
        P(),
    )
    out_specs = (P(None, None, "ctx"), P("ctx", None, "tp", None))
    return jax.shard_map(body, mesh=mesh, in_specs=in_specs, out_specs=out_specs, check_vma=False)
```

```python
import functools
import math

import jax
import jax.numpy as jnp
import numpy as np
from jax import lax
from jax.experimental import pallas as pl
from jax.experimental.pallas import tpu as pltpu
from jax.sharding import PartitionSpec as P

MESH = pl.DeviceIdType.MESH
ZN, XN, TP = 16, 4, 8
HEADS = 8
LOW = -1e30
VL = 60


def remote(src, dst, send, recv, target):
    return pltpu.make_async_remote_copy(
        src_ref=src,
        dst_ref=dst,
        send_sem=send,
        recv_sem=recv,
        device_id=target,
        device_id_type=MESH,
    )


def wait_bytes(ref, sem):
    pltpu.make_async_copy(ref, ref, sem).wait()


def swap_halves(values, axis):
    return pltpu.roll(values, 64, axis)


def kernel(
    len_ref, hid_hbm, gain_hbm, inv_hbm, own_hbm, tgt_hbm, wq_hbm, wo_hbm, cache_hbm,
    att_ref, rel_ref,
    hid_ref, gain_ref, inv_ref, own_ref, tgt, slot_v, slot_s, wq, wo, cache, packed,
    hid32, pbuf, xbuf, zsend, zbuf, asend, gbuf, kvs,
    bbuf, zb2, x2send, x2buf, ats, agb, osend, tbuf, fs,
    in_sem, own_sem, a2a_send, a2a_recv, chain_send, chain_recv, ready,
):
    me = lax.axis_index("ctx")
    mt = lax.axis_index("tp")
    z = me // XN
    x = me % XN

    def at_z(dz):
        return ((z + dz) % ZN) * XN + x

    def at_x(dx):
        return z * XN + (x + dx) % XN

    barrier = pltpu.get_barrier_semaphore()

    def greet(dz, dx):
        to = ((z + dz + ZN) % ZN) * XN + (x + dx) % XN
        pl.semaphore_signal(barrier, inc=1, device_id={"ctx": to}, device_id_type=MESH)

    def greet_both(step, carry):
        for dx in range(XN):
            greet(4 - step, dx)
            greet(step - 4, dx)
        return carry

    def greet_tp(k, carry):
        pl.semaphore_signal(barrier, inc=1, device_id={"tp": (mt + k) % TP}, device_id_type=MESH)
        return carry

    lax.fori_loop(0, 4, greet_both, 0)
    for dx in range(1, XN):
        greet(0, dx)
    lax.fori_loop(1, TP, greet_tp, 0)

    cp_tgt = pltpu.make_async_copy(tgt_hbm.at[me], tgt, in_sem.at[0])
    cp_wq = pltpu.make_async_copy(wq_hbm, wq, in_sem.at[1])
    cp_cache = pltpu.make_async_copy(cache_hbm, cache, in_sem.at[2])
    cp_wo = pltpu.make_async_copy(wo_hbm, wo, in_sem.at[3])
    cp_hid = pltpu.make_async_copy(hid_hbm, hid_ref, in_sem.at[5])
    cp_gain = pltpu.make_async_copy(gain_hbm, gain_ref, in_sem.at[6])
    cp_inv = pltpu.make_async_copy(inv_hbm, inv_ref, in_sem.at[7])
    cp_own_dev = pltpu.make_async_copy(own_hbm, own_ref, in_sem.at[8])
    cp_tgt.start()
    cp_hid.start()
    cp_gain.start()
    cp_wq.start()
    cp_cache.start()
    cp_inv.start()
    cp_own_dev.start()
    cp_wo.start()

    hid32[...] = jnp.zeros_like(hid32)
    cp_hid.wait()
    cp_gain.wait()
    for step in range(3):
        hid32[4 * step : 4 * step + 4, :] = hid_ref[step].astype(jnp.float32)
    hidden = hid32[...]
    scaled = (hidden * gain_ref[...]).astype(jnp.bfloat16)
    row16 = lax.broadcasted_iota(jnp.int32, (16, 128), 0)
    lane16 = lax.broadcasted_iota(jnp.int32, (16, 128), 1)
    squares = jnp.sum(hidden * hidden, axis=1, keepdims=True)
    square_row = jnp.sum(jnp.where(row16 == lane16, squares, 0.0), axis=0, keepdims=True)
    row8 = lax.broadcasted_iota(jnp.int32, (8, 128), 0)
    lane8 = lax.broadcasted_iota(jnp.int32, (8, 128), 1)
    pbuf[120:128, :] = jnp.where(row8 == 0, square_row, 0.0)
    cp_wq.wait()
    for head in range(HEADS + 2):
        part = jnp.dot(
            scaled, wq[:, 128 * head : 128 * head + 128], preferred_element_type=jnp.float32
        )
        pbuf[12 * head : 12 * head + 12, :] = part[0:12, :]

    cp_tgt.wait()
    t_iota = lax.broadcasted_iota(jnp.int32, (64, 128), 0)
    b_iota = lax.broadcasted_iota(jnp.int32, (64, 128), 1)
    match = tgt[...] == t_iota
    first = jnp.min(jnp.where(match, b_iota, 127), axis=1, keepdims=True)
    last = jnp.max(jnp.where(match, b_iota, 0), axis=1, keepdims=True)
    slot_v[...] = jnp.where(b_iota == 0, first, last)
    cp_slot = pltpu.make_async_copy(slot_v, slot_s, in_sem.at[4])
    cp_slot.start()
    def send_blocks(dz, dx):
        to = ((z + dz + ZN) % ZN) * XN + (x + dx) % XN
        remote(
            packed.at[pl.ds(2 * to, 2)], rel_ref.at[mine], a2a_send, a2a_recv, {"ctx": to}
        ).start()

    def bulk(slot):
        for shifts, low, high in PLAN[slot]:

            def one(dx, carry):
                for dz in shifts:
                    send_blocks(dz, dx)
                return carry

            lax.fori_loop(low, high, one, 0)

    def far_first(send):
        def both_ways(step, carry):
            send(ZN // 2 + step)
            send(ZN // 2 - step)
            return carry

        send(ZN // 2)
        lax.fori_loop(1, ZN // 2, both_ways, 0)

    cp_slot.wait()
    cp_cache.wait()

    def pack(t, carry):
        packed[2 * t] = cache[slot_s[t, 0]]
        packed[2 * t + 1] = cache[slot_s[t, 1]]
        return carry

    lax.fori_loop(0, ZN * XN, pack, 0)
    mine = pl.ds(2 * me, 2)
    cp_own = pltpu.make_async_copy(packed.at[mine], rel_ref.at[mine], own_sem)
    cp_own.start()

    pl.semaphore_wait(barrier, 9 * XN - 1 + TP - 1)
    for dz in (4, -4):
        pl.semaphore_signal(ready, inc=1, device_id={"ctx": at_z(dz + ZN)}, device_id_type=MESH)

    quarter = pl.ds(pl.multiple_of(32 * x, 32), 32)
    for dx in (2, 1, 3):
        to = (x + dx) % XN
        remote(
            pbuf.at[pl.ds(pl.multiple_of(32 * to, 32), 32)], xbuf.at[x],
            chain_send.at[0], chain_recv.at[0], {"ctx": at_x(dx)},
        ).start()

    bulk(0)
    xbuf[x] = pbuf[quarter, :]
    wait_bytes(xbuf.at[pl.ds(0, XN - 1)], chain_recv.at[0])
    total = jnp.sum(xbuf[...], axis=0)
    pl.semaphore_wait(ready, 2)
    zsend[...] = total.reshape(4, 8, 128)
    chunk = z % 4

    def scatter_a(dz):
        to = (z + dz) % ZN
        remote(
            zsend.at[to % 4], zbuf.at[z], chain_send.at[1], chain_recv.at[1], {"ctx": to * XN + x}
        ).start()

    far_first(scatter_a)
    bulk(1)

    row24 = lax.broadcasted_iota(jnp.int32, (24, 128), 0)
    lane24 = lax.broadcasted_iota(jnp.int32, (24, 128), 1)
    seq24 = row24 % 4
    row_in = row24 % 12
    length24 = jnp.where(
        seq24 == 0,
        len_ref[0],
        jnp.where(seq24 == 1, len_ref[1], jnp.where(seq24 == 2, len_ref[2], len_ref[3])),
    )
    position = length24.astype(jnp.float32) + (row_in // 4).astype(jnp.float32)
    cp_inv.wait()
    angle = position * inv_ref[...]
    cosine = jnp.cos(angle)
    sine = jnp.where(lane24 < 64, -jnp.sin(angle), jnp.sin(angle))

    cp_own_dev.wait()
    own_iota = lax.broadcasted_iota(jnp.int32, (1, 64), 1)
    segment = jnp.sum(jnp.where(own_ref[...] == me, own_iota, 0), axis=1, keepdims=True)
    my_seq = segment // 16
    my_offset = segment % 16 * 2048
    my_length = jnp.where(
        my_seq == 0,
        len_ref[0],
        jnp.where(my_seq == 1, len_ref[1], jnp.where(my_seq == 2, len_ref[2], len_ref[3])),
    )

    zbuf[z] = zsend[chunk]
    wait_bytes(zbuf.at[pl.ds(0, ZN - 1)], chain_recv.at[1])
    total = jnp.sum(zbuf[...], axis=0)
    asend[...] = total
    gbuf[x, chunk] = total
    for dz, dx in ((2, 2), (2, 1), (2, 3), (1, 2), (-1, 2), (1, 1), (-1, 1), (1, 3), (-1, 3),
                   (2, 0), (0, 2), (1, 0), (-1, 0), (0, 1), (0, 3)):
        to = ((z + dz + ZN) % ZN) * XN + (x + dx) % XN
        remote(
            asend, gbuf.at[x, chunk], chain_send.at[2], chain_recv.at[2], {"ctx": to}
        ).start()
    bulk(2)
    wait_bytes(zbuf.at[pl.ds(0, 15)], chain_recv.at[2])

    whole = gbuf[...].reshape(128, 128)
    square_sum = jnp.sum(
        jnp.where(lane24 == row_in, whole[120:121, :], 0.0), axis=1, keepdims=True
    )
    norm = jnp.sqrt(square_sum / 8192.0 + 1e-05)
    rotated = []
    for g in range(5):
        plain = whole[24 * g : 24 * g + 24, :] / norm
        turned = plain * cosine + swap_halves(plain, 1) * sine
        if g < 4:
            rotated.append(turned)
        else:
            kvs[0:24, :] = jnp.where(row24 < 12, turned, plain)
    kvs[24:32, :] = jnp.zeros((8, 128), jnp.float32)
    queries = jnp.concatenate(rotated, axis=0).astype(jnp.bfloat16)

    pick_row = lax.broadcasted_iota(jnp.int32, (32, 96), 0)
    pick_col = lax.broadcasted_iota(jnp.int32, (32, 96), 1)
    wanted = 12 * (pick_row // 4) + 4 * (pick_row % 4) + my_seq
    pick = jnp.where((wanted == pick_col) & (pick_row % 4 < 3), 1.0, 0.0).astype(jnp.bfloat16)
    my_queries = jnp.dot(pick, queries, preferred_element_type=jnp.float32).astype(jnp.bfloat16)
    keys = cache[:, :, 0:128].reshape(2048, 128)
    values = cache[:, :, 128:256].reshape(2048, 128)
    scale = 1.0 / math.sqrt(128)
    scores = (
        lax.dot_general(
            my_queries, keys, (((1,), (1,)), ((), ())), preferred_element_type=jnp.float32
        )
        * scale
    )
    place = my_offset + lax.broadcasted_iota(jnp.int32, (1, 2048), 1)
    live = place < my_length
    scores = jnp.where(live, scores, LOW)
    highest = jnp.max(scores, axis=1, keepdims=True)
    weights = jnp.where(live, jnp.exp(scores - highest), 0.0)
    weight_sum = jnp.sum(weights, axis=1, keepdims=True)
    weighted = jnp.dot(weights.astype(jnp.bfloat16), values, preferred_element_type=jnp.float32)
    row32 = lax.broadcasted_iota(jnp.int32, (32, 128), 0) % 4
    lane32 = lax.broadcasted_iota(jnp.int32, (32, 128), 1)
    stats = jnp.where(lane32 < 3, highest, weight_sum)
    placed = my_seq.astype(jnp.float32)
    for step in range(3):
        shifted = pltpu.roll(stats, 3 - step, 0)
        placed = jnp.where((lane32 == step) | (lane32 == 3 + step), shifted, placed)
    partial = jnp.where(row32 < 3, weighted, placed)
    for h in range(HEADS):
        bbuf[h] = partial[4 * h : 4 * h + 4, :]

    head = z % HEADS

    def scatter_b(dz):
        to = (z + dz) % ZN
        remote(
            bbuf.at[to % HEADS], zb2.at[z], chain_send.at[3], chain_recv.at[3], {"ctx": to * XN + x}
        ).start()

    far_first(scatter_b)
    bulk(3)
    zb2[z] = bbuf[head]

    pick_row = lax.broadcasted_iota(jnp.int32, (16, 96), 0)
    pick_col = lax.broadcasted_iota(jnp.int32, (16, 96), 1)
    wanted = 12 * head + 4 * (pick_row % 3) + pick_row // 3
    pick = jnp.where((wanted == pick_col) & (pick_row < 12), 1.0, 0.0).astype(jnp.bfloat16)
    head_queries = jnp.dot(pick, queries, preferred_element_type=jnp.float32).astype(jnp.bfloat16)
    new_keys = kvs[0:16, :].astype(jnp.bfloat16)
    new_values = kvs[12:28, :].astype(jnp.bfloat16)
    fresh = (
        lax.dot_general(
            head_queries, new_keys, (((1,), (1,)), ((), ())), preferred_element_type=jnp.float32
        )
        * scale
    )
    q_row = lax.broadcasted_iota(jnp.int32, (16, 16), 0)
    k_col = lax.broadcasted_iota(jnp.int32, (16, 16), 1)
    seen = (
        (q_row // 3 == k_col % 4) & (k_col // 4 <= q_row % 3) & (k_col < 12) & (q_row < 12)
    )
    fresh = jnp.where(seen, fresh, LOW)
    fresh_high = jnp.max(fresh, axis=1, keepdims=True)
    x2send[...] = jnp.where(lax.broadcasted_iota(jnp.int32, (32, 128), 0) < 16, 0.0, 1.0)

    wait_bytes(zb2.at[pl.ds(0, ZN - 1)], chain_recv.at[3])
    stats = zb2[:, 3, :]
    part_sum = pltpu.roll(stats, 125, 1)
    part_seq = stats[:, 6:7]
    lane1 = lax.broadcasted_iota(jnp.int32, (1, 128), 1)
    for seq in range(4):
        member = part_seq == float(seq)
        high = jnp.max(jnp.where(member, stats, LOW), axis=0, keepdims=True)
        factor = jnp.where(member, jnp.exp(stats - high), 0.0)
        sums = jnp.sum(factor * part_sum, axis=0, keepdims=True)
        for step in range(3):
            r = 3 * seq + step
            accs = jnp.sum(factor[:, step : step + 1] * zb2[:, step, :], axis=0, keepdims=True)
            x2send[r : r + 1, :] = accs
            x2send[16 + r : 17 + r, :] = jnp.where(
                lane1 < 64, high[:, step : step + 1], sums[:, step : step + 1]
            )
    x2buf[x] = x2send[...]
    for dx in (2, 1, 3):
        remote(
            x2send, x2buf.at[x], chain_send.at[4], chain_recv.at[4], {"ctx": at_x(dx)}
        ).start()
    bulk(4)
    wait_bytes(x2buf.at[pl.ds(0, XN - 1)], chain_recv.at[4])
    accs = x2buf[:, 0:16, :]
    stats = x2buf[:, 16:32, :]
    lane_x = lax.broadcasted_iota(jnp.int32, (4, 16, 128), 2)
    turned = swap_halves(stats, 2)
    part_high = jnp.where(lane_x < 64, stats, turned)
    part_sum = jnp.where(lane_x < 64, turned, stats)
    high = jnp.maximum(jnp.max(part_high, axis=0), fresh_high)
    factor = jnp.exp(part_high - high[None])
    fresh_weights = jnp.where(seen, jnp.exp(fresh - high[:, 0:1]), 0.0)
    sums = jnp.sum(factor * part_sum, axis=0) + jnp.sum(fresh_weights, axis=1, keepdims=True)
    mixed = jnp.sum(factor * accs, axis=0) + jnp.dot(
        fresh_weights.astype(jnp.bfloat16), new_values, preferred_element_type=jnp.float32
    )
    attention = (mixed / sums).astype(jnp.bfloat16)
    ats[...] = attention
    agb[head] = attention
    for dz in (4, 3, -3, 2, -2, 1, -1):
        remote(
            ats, agb.at[head], chain_send.at[5], chain_recv.at[5], {"ctx": at_z(dz + ZN)}
        ).start()
    bulk(5)
    cp_wo.wait()
    wait_bytes(agb.at[pl.ds(0, HEADS - 1)], chain_recv.at[5])

    out = jnp.zeros((16, 128), jnp.float32)
    for h in range(HEADS):
        out = out + jnp.dot(
            agb[h], wo[128 * h : 128 * h + 128, :], preferred_element_type=jnp.float32
        )
    osend[...] = out
    tbuf[mt] = out
    for dt in (4, 5, 3, 2, 6, 1, 7):
        remote(
            osend, tbuf.at[mt], chain_send.at[6], chain_recv.at[6], {"tp": (mt + dt) % TP}
        ).start()
    bulk(6)
    wait_bytes(tbuf.at[pl.ds(0, TP - 1)], chain_recv.at[6])
    out = jnp.sum(tbuf[...], axis=0)
    for step in range(3):
        for seq in range(4):
            r = 3 * seq + step
            fs[step, seq : seq + 1, :] = out[r : r + 1, :]
    att_ref[...] = fs[...].astype(jnp.bfloat16)

    wait_bytes(xbuf.at[pl.ds(0, XN - 1)], chain_send.at[0])
    wait_bytes(zbuf.at[pl.ds(0, ZN - 1)], chain_send.at[1])
    wait_bytes(zbuf.at[pl.ds(0, 15)], chain_send.at[2])
    wait_bytes(zb2.at[pl.ds(0, ZN - 1)], chain_send.at[3])
    wait_bytes(x2buf.at[pl.ds(0, XN - 1)], chain_send.at[4])
    wait_bytes(agb.at[pl.ds(0, HEADS - 1)], chain_send.at[5])
    wait_bytes(tbuf.at[pl.ds(0, TP - 1)], chain_send.at[6])
    cp_own.wait()
    others = pl.ds(0, 2 * (ZN * XN - 1))
    wait_bytes(packed.at[others], a2a_send)
    wait_bytes(rel_ref.at[others], a2a_recv)


NEAR = (((1, -1, 2, -2), 0, 4), ((0,), 1, 4))
PLAN = (NEAR, (((8,), 0, 4), ((7, -7), 0, 2)), (((7, -7), 2, 4),), (((6, -6), 0, 4), ((5, -5), 0, 4)), (), (((4, -4), 0, 4), ((3, -3), 0, 4)), ())


def inverse_table():
    half = np.arange(64, dtype=np.float32)
    power = np.float32(-math.log(500000.0)) * half * np.float32(2.0) / np.float32(128.0)
    inverse = np.exp(power.astype(np.float64)).astype(np.float32)
    return np.concatenate([inverse, inverse])[None, :]


def body(
    new_hidden, norm_gain, qkv_weight, out_weight, owned_cache, lengths, owner_device, block_target
):
    f32, bf16, i32 = jnp.float32, jnp.bfloat16, jnp.int32
    vmem = pl.BlockSpec(memory_space=pltpu.VMEM)
    smem = pl.BlockSpec(memory_space=pltpu.SMEM)
    hbm = pl.BlockSpec(memory_space=pltpu.HBM)
    dma = pltpu.SemaphoreType.DMA
    attended, relaid = pl.pallas_call(
        kernel,
        out_shape=(
            pltpu.VMEM((3, 4, 128), bf16),
            pltpu.VMEM((128, 16, 256), bf16),
        ),
        in_specs=[smem] + [hbm] * 8,
        out_specs=(vmem, vmem),
        scratch_shapes=[
            pltpu.VMEM((3, 4, 128), bf16),
            pltpu.VMEM((1, 128), f32),
            pltpu.VMEM((1, 128), f32),
            pltpu.VMEM((1, 64), i32),
            pltpu.VMEM((1, 128), i32),
            pltpu.VMEM((64, 128), i32),
            pltpu.SMEM((64, 128), i32),
            pltpu.VMEM((128, 1280), bf16),
            pltpu.VMEM((1024, 128), bf16),
            pltpu.VMEM((128, 16, 256), bf16),
            pltpu.VMEM((128, 16, 256), bf16),
            pltpu.VMEM((16, 128), f32),
            pltpu.VMEM((128, 128), f32),
            pltpu.VMEM((4, 32, 128), f32),
            pltpu.VMEM((4, 8, 128), f32),
            pltpu.VMEM((16, 8, 128), f32),
            pltpu.VMEM((8, 128), f32),
            pltpu.VMEM((4, 4, 8, 128), f32),
            pltpu.VMEM((32, 128), f32),
            pltpu.VMEM((8, 4, 128), f32),
            pltpu.VMEM((16, 4, 128), f32),
            pltpu.VMEM((32, 128), f32),
            pltpu.VMEM((4, 32, 128), f32),
            pltpu.VMEM((16, 128), bf16),
            pltpu.VMEM((8, 16, 128), bf16),
            pltpu.VMEM((16, 128), f32),
            pltpu.VMEM((8, 16, 128), f32),
            pltpu.VMEM((3, 4, 128), f32),
            dma((9,)),
            dma,
            dma,
            dma,
            dma((7,)),
            dma((7,)),
            pltpu.SemaphoreType.REGULAR,
        ],
        compiler_params=pltpu.CompilerParams(
            collective_id=0, has_side_effects=True, vmem_limit_bytes=VL * 1024 * 1024
        ),
        name="decode_and_relay",
    )(
        lengths,
        new_hidden,
        norm_gain.reshape(1, 128),
        jnp.asarray(inverse_table()),
        owner_device.reshape(1, 64),
        block_target.reshape(64, 1, 128),
        qkv_weight.reshape(128, 1280),
        out_weight.reshape(1024, 128),
        owned_cache.reshape(128, 16, 256),
    )
    return attended, relaid.reshape(128, 16, 1, 256)


def solution(mesh):
    in_specs = (
        P(None, None, "ctx"),
        P("ctx"),
        P("ctx", "tp", None),
        P("tp", None, "ctx"),
        P("ctx", None, "tp", None),
        P(),
        P(),
        P(),
    )
    out_specs = (P(None, None, "ctx"), P("ctx", None, "tp", None))
    return jax.shard_map(body, mesh=mesh, in_specs=in_specs, out_specs=out_specs, check_vma=False)
```

```python
import functools
import math

import jax
import jax.numpy as jnp
import numpy as np
from jax import lax
from jax.experimental import pallas as pl
from jax.experimental.pallas import tpu as pltpu
from jax.sharding import PartitionSpec as P

MESH = pl.DeviceIdType.MESH
ZN, XN, TP = 16, 4, 8
HEADS = 8
LOW = -1e30
VL = 60


def remote(src, dst, send, recv, target):
    return pltpu.make_async_remote_copy(
        src_ref=src,
        dst_ref=dst,
        send_sem=send,
        recv_sem=recv,
        device_id=target,
        device_id_type=MESH,
    )


def wait_bytes(ref, sem):
    pltpu.make_async_copy(ref, ref, sem).wait()


def swap_halves(values, axis):
    return pltpu.roll(values, 64, axis)


def kernel(
    len_ref, hid_hbm, gain_hbm, inv_hbm, own_hbm, tgt_hbm, wq_hbm, wo_hbm, cache_hbm,
    att_ref, rel_ref,
    hid_ref, gain_ref, inv_ref, own_ref, tgt, slot_v, slot_s, wq, wo, cache, packed,
    hid32, pbuf, xbuf, zsend, zbuf, asend, gbuf, kvs,
    bbuf, zb2, x2send, x2buf, ats, agb, osend, tbuf, fs,
    in_sem, own_sem, a2a_send, a2a_recv, chain_send, chain_recv, ready,
):
    me = lax.axis_index("ctx")
    mt = lax.axis_index("tp")
    z = me // XN
    x = me % XN

    def at_z(dz):
        return ((z + dz) % ZN) * XN + x

    def at_x(dx):
        return z * XN + (x + dx) % XN

    cp_tgt = pltpu.make_async_copy(tgt_hbm.at[me], tgt, in_sem.at[0])
    cp_wq = pltpu.make_async_copy(wq_hbm, wq, in_sem.at[1])
    cp_cache = pltpu.make_async_copy(cache_hbm, cache, in_sem.at[2])
    cp_wo = pltpu.make_async_copy(wo_hbm, wo, in_sem.at[3])
    cp_hid = pltpu.make_async_copy(hid_hbm, hid_ref, in_sem.at[5])
    cp_gain = pltpu.make_async_copy(gain_hbm, gain_ref, in_sem.at[6])
    cp_inv = pltpu.make_async_copy(inv_hbm, inv_ref, in_sem.at[7])
    cp_own_dev = pltpu.make_async_copy(own_hbm, own_ref, in_sem.at[8])
    cp_tgt.start()
    cp_hid.start()
    cp_gain.start()
    cp_wq.start()
    cp_cache.start()
    cp_inv.start()
    cp_own_dev.start()
    cp_wo.start()

    barrier = pltpu.get_barrier_semaphore()

    def greet(dz, dx):
        to = ((z + dz + ZN) % ZN) * XN + (x + dx) % XN
        pl.semaphore_signal(barrier, inc=1, device_id={"ctx": to}, device_id_type=MESH)

    def greet_both(step, carry):
        for dx in range(XN):
            greet(4 - step, dx)
            greet(step - 4, dx)
        return carry

    def greet_tp(k, carry):
        pl.semaphore_signal(barrier, inc=1, device_id={"tp": (mt + k) % TP}, device_id_type=MESH)
        return carry

    lax.fori_loop(0, 4, greet_both, 0)
    for dx in range(1, XN):
        greet(0, dx)
    lax.fori_loop(1, TP, greet_tp, 0)

    cp_tgt.wait()
    t_iota = lax.broadcasted_iota(jnp.int32, (64, 128), 0)
    b_iota = lax.broadcasted_iota(jnp.int32, (64, 128), 1)
    match = tgt[...] == t_iota
    first = jnp.min(jnp.where(match, b_iota, 127), axis=1, keepdims=True)
    last = jnp.max(jnp.where(match, b_iota, 0), axis=1, keepdims=True)
    slot_v[...] = jnp.where(b_iota == 0, first, last)
    cp_slot = pltpu.make_async_copy(slot_v, slot_s, in_sem.at[4])
    cp_slot.start()
    def send_blocks(dz, dx):
        to = ((z + dz + ZN) % ZN) * XN + (x + dx) % XN
        remote(
            packed.at[pl.ds(2 * to, 2)], rel_ref.at[mine], a2a_send, a2a_recv, {"ctx": to}
        ).start()

    def bulk(slot):
        for shifts, low, high in PLAN[slot]:

            def one(dx, carry):
                for dz in shifts:
                    send_blocks(dz, dx)
                return carry

            lax.fori_loop(low, high, one, 0)

    def far_first(send):
        def both_ways(step, carry):
            send(ZN // 2 + step)
            send(ZN // 2 - step)
            return carry

        send(ZN // 2)
        lax.fori_loop(1, ZN // 2, both_ways, 0)


    hid32[...] = jnp.zeros_like(hid32)
    cp_hid.wait()
    cp_gain.wait()
    for step in range(3):
        hid32[4 * step : 4 * step + 4, :] = hid_ref[step].astype(jnp.float32)
    hidden = hid32[...]
    scaled = (hidden * gain_ref[...]).astype(jnp.bfloat16)
    row16 = lax.broadcasted_iota(jnp.int32, (16, 128), 0)
    lane16 = lax.broadcasted_iota(jnp.int32, (16, 128), 1)
    squares = jnp.sum(hidden * hidden, axis=1, keepdims=True)
    square_row = jnp.sum(jnp.where(row16 == lane16, squares, 0.0), axis=0, keepdims=True)
    row8 = lax.broadcasted_iota(jnp.int32, (8, 128), 0)
    lane8 = lax.broadcasted_iota(jnp.int32, (8, 128), 1)
    pbuf[120:128, :] = jnp.where(row8 == 0, square_row, 0.0)
    cp_wq.wait()
    for head in range(HEADS + 2):
        part = jnp.dot(
            scaled, wq[:, 128 * head : 128 * head + 128], preferred_element_type=jnp.float32
        )
        pbuf[12 * head : 12 * head + 12, :] = part[0:12, :]

    cp_slot.wait()
    cp_cache.wait()

    def pack(t, carry):
        packed[2 * t] = cache[slot_s[t, 0]]
        packed[2 * t + 1] = cache[slot_s[t, 1]]
        return carry

    lax.fori_loop(0, ZN * XN, pack, 0)
    mine = pl.ds(2 * me, 2)
    cp_own = pltpu.make_async_copy(packed.at[mine], rel_ref.at[mine], own_sem)
    cp_own.start()

    pl.semaphore_wait(barrier, 9 * XN - 1 + TP - 1)
    for dz in (4, -4):
        pl.semaphore_signal(ready, inc=1, device_id={"ctx": at_z(dz + ZN)}, device_id_type=MESH)

    quarter = pl.ds(pl.multiple_of(32 * x, 32), 32)
    for dx in (2, 1, 3):
        to = (x + dx) % XN
        remote(
            pbuf.at[pl.ds(pl.multiple_of(32 * to, 32), 32)], xbuf.at[x],
            chain_send.at[0], chain_recv.at[0], {"ctx": at_x(dx)},
        ).start()

    bulk(0)
    xbuf[x] = pbuf[quarter, :]
    wait_bytes(xbuf.at[pl.ds(0, XN - 1)], chain_recv.at[0])
    total = jnp.sum(xbuf[...], axis=0)
    pl.semaphore_wait(ready, 2)
    zsend[...] = total.reshape(4, 8, 128)
    chunk = z % 4

    def scatter_a(dz):
        to = (z + dz) % ZN
        remote(
            zsend.at[to % 4], zbuf.at[z], chain_send.at[1], chain_recv.at[1], {"ctx": to * XN + x}
        ).start()

    far_first(scatter_a)
    bulk(1)

    row24 = lax.broadcasted_iota(jnp.int32, (24, 128), 0)
    lane24 = lax.broadcasted_iota(jnp.int32, (24, 128), 1)
    seq24 = row24 % 4
    row_in = row24 % 12
    length24 = jnp.where(
        seq24 == 0,
        len_ref[0],
        jnp.where(seq24 == 1, len_ref[1], jnp.where(seq24 == 2, len_ref[2], len_ref[3])),
    )
    position = length24.astype(jnp.float32) + (row_in // 4).astype(jnp.float32)
    cp_inv.wait()
    angle = position * inv_ref[...]
    cosine = jnp.cos(angle)
    sine = jnp.where(lane24 < 64, -jnp.sin(angle), jnp.sin(angle))

    cp_own_dev.wait()
    own_iota = lax.broadcasted_iota(jnp.int32, (1, 64), 1)
    segment = jnp.sum(jnp.where(own_ref[...] == me, own_iota, 0), axis=1, keepdims=True)
    my_seq = segment // 16
    my_offset = segment % 16 * 2048
    my_length = jnp.where(
        my_seq == 0,
        len_ref[0],
        jnp.where(my_seq == 1, len_ref[1], jnp.where(my_seq == 2, len_ref[2], len_ref[3])),
    )

    zbuf[z] = zsend[chunk]
    wait_bytes(zbuf.at[pl.ds(0, ZN - 1)], chain_recv.at[1])
    total = jnp.sum(zbuf[...], axis=0)
    asend[...] = total
    gbuf[x, chunk] = total
    for dz, dx in ((2, 2), (2, 1), (2, 3), (1, 2), (-1, 2), (1, 1), (-1, 1), (1, 3), (-1, 3),
                   (2, 0), (0, 2), (1, 0), (-1, 0), (0, 1), (0, 3)):
        to = ((z + dz + ZN) % ZN) * XN + (x + dx) % XN
        remote(
            asend, gbuf.at[x, chunk], chain_send.at[2], chain_recv.at[2], {"ctx": to}
        ).start()
    bulk(2)
    wait_bytes(zbuf.at[pl.ds(0, 15)], chain_recv.at[2])

    whole = gbuf[...].reshape(128, 128)
    square_sum = jnp.sum(
        jnp.where(lane24 == row_in, whole[120:121, :], 0.0), axis=1, keepdims=True
    )
    norm = jnp.sqrt(square_sum / 8192.0 + 1e-05)
    rotated = []
    for g in range(5):
        plain = whole[24 * g : 24 * g + 24, :] / norm
        turned = plain * cosine + swap_halves(plain, 1) * sine
        if g < 4:
            rotated.append(turned)
        else:
            kvs[0:24, :] = jnp.where(row24 < 12, turned, plain)
    kvs[24:32, :] = jnp.zeros((8, 128), jnp.float32)
    queries = jnp.concatenate(rotated, axis=0).astype(jnp.bfloat16)

    pick_row = lax.broadcasted_iota(jnp.int32, (32, 96), 0)
    pick_col = lax.broadcasted_iota(jnp.int32, (32, 96), 1)
    wanted = 12 * (pick_row // 4) + 4 * (pick_row % 4) + my_seq
    pick = jnp.where((wanted == pick_col) & (pick_row % 4 < 3), 1.0, 0.0).astype(jnp.bfloat16)
    my_queries = jnp.dot(pick, queries, preferred_element_type=jnp.float32).astype(jnp.bfloat16)
    keys = cache[:, :, 0:128].reshape(2048, 128)
    values = cache[:, :, 128:256].reshape(2048, 128)
    scale = 1.0 / math.sqrt(128)
    scores = (
        lax.dot_general(
            my_queries, keys, (((1,), (1,)), ((), ())), preferred_element_type=jnp.float32
        )
        * scale
    )
    place = my_offset + lax.broadcasted_iota(jnp.int32, (1, 2048), 1)
    live = place < my_length
    scores = jnp.where(live, scores, LOW)
    highest = jnp.max(scores, axis=1, keepdims=True)
    weights = jnp.where(live, jnp.exp(scores - highest), 0.0)
    weight_sum = jnp.sum(weights, axis=1, keepdims=True)
    weighted = jnp.dot(weights.astype(jnp.bfloat16), values, preferred_element_type=jnp.float32)
    row32 = lax.broadcasted_iota(jnp.int32, (32, 128), 0) % 4
    lane32 = lax.broadcasted_iota(jnp.int32, (32, 128), 1)
    stats = jnp.where(lane32 < 3, highest, weight_sum)
    placed = my_seq.astype(jnp.float32)
    for step in range(3):
        shifted = pltpu.roll(stats, 3 - step, 0)
        placed = jnp.where((lane32 == step) | (lane32 == 3 + step), shifted, placed)
    partial = jnp.where(row32 < 3, weighted, placed)
    for h in range(HEADS):
        bbuf[h] = partial[4 * h : 4 * h + 4, :]

    head = z % HEADS

    def scatter_b(dz):
        to = (z + dz) % ZN
        remote(
            bbuf.at[to % HEADS], zb2.at[z], chain_send.at[3], chain_recv.at[3], {"ctx": to * XN + x}
        ).start()

    far_first(scatter_b)
    bulk(3)
    zb2[z] = bbuf[head]

    pick_row = lax.broadcasted_iota(jnp.int32, (16, 96), 0)
    pick_col = lax.broadcasted_iota(jnp.int32, (16, 96), 1)
    wanted = 12 * head + 4 * (pick_row % 3) + pick_row // 3
    pick = jnp.where((wanted == pick_col) & (pick_row < 12), 1.0, 0.0).astype(jnp.bfloat16)
    head_queries = jnp.dot(pick, queries, preferred_element_type=jnp.float32).astype(jnp.bfloat16)
    new_keys = kvs[0:16, :].astype(jnp.bfloat16)
    new_values = kvs[12:28, :].astype(jnp.bfloat16)
    fresh = (
        lax.dot_general(
            head_queries, new_keys, (((1,), (1,)), ((), ())), preferred_element_type=jnp.float32
        )
        * scale
    )
    q_row = lax.broadcasted_iota(jnp.int32, (16, 16), 0)
    k_col = lax.broadcasted_iota(jnp.int32, (16, 16), 1)
    seen = (
        (q_row // 3 == k_col % 4) & (k_col // 4 <= q_row % 3) & (k_col < 12) & (q_row < 12)
    )
    fresh = jnp.where(seen, fresh, LOW)
    fresh_high = jnp.max(fresh, axis=1, keepdims=True)
    x2send[...] = jnp.where(lax.broadcasted_iota(jnp.int32, (32, 128), 0) < 16, 0.0, 1.0)

    wait_bytes(zb2.at[pl.ds(0, ZN - 1)], chain_recv.at[3])
    stats = zb2[:, 3, :]
    part_sum = pltpu.roll(stats, 125, 1)
    part_seq = stats[:, 6:7]
    lane1 = lax.broadcasted_iota(jnp.int32, (1, 128), 1)
    for seq in range(4):
        member = part_seq == float(seq)
        high = jnp.max(jnp.where(member, stats, LOW), axis=0, keepdims=True)
        factor = jnp.where(member, jnp.exp(stats - high), 0.0)
        sums = jnp.sum(factor * part_sum, axis=0, keepdims=True)
        for step in range(3):
            r = 3 * seq + step
            accs = jnp.sum(factor[:, step : step + 1] * zb2[:, step, :], axis=0, keepdims=True)
            x2send[r : r + 1, :] = accs
            x2send[16 + r : 17 + r, :] = jnp.where(
                lane1 < 64, high[:, step : step + 1], sums[:, step : step + 1]
            )
    x2buf[x] = x2send[...]
    for dx in (2, 1, 3):
        remote(
            x2send, x2buf.at[x], chain_send.at[4], chain_recv.at[4], {"ctx": at_x(dx)}
        ).start()
    bulk(4)
    wait_bytes(x2buf.at[pl.ds(0, XN - 1)], chain_recv.at[4])
    accs = x2buf[:, 0:16, :]
    stats = x2buf[:, 16:32, :]
    lane_x = lax.broadcasted_iota(jnp.int32, (4, 16, 128), 2)
    turned = swap_halves(stats, 2)
    part_high = jnp.where(lane_x < 64, stats, turned)
    part_sum = jnp.where(lane_x < 64, turned, stats)
    high = jnp.maximum(jnp.max(part_high, axis=0), fresh_high)
    factor = jnp.exp(part_high - high[None])
    fresh_weights = jnp.where(seen, jnp.exp(fresh - high[:, 0:1]), 0.0)
    sums = jnp.sum(factor * part_sum, axis=0) + jnp.sum(fresh_weights, axis=1, keepdims=True)
    mixed = jnp.sum(factor * accs, axis=0) + jnp.dot(
        fresh_weights.astype(jnp.bfloat16), new_values, preferred_element_type=jnp.float32
    )
    attention = (mixed / sums).astype(jnp.bfloat16)
    ats[...] = attention
    agb[head] = attention
    for dz in (4, 3, -3, 2, -2, 1, -1):
        remote(
            ats, agb.at[head], chain_send.at[5], chain_recv.at[5], {"ctx": at_z(dz + ZN)}
        ).start()
    bulk(5)
    cp_wo.wait()
    wait_bytes(agb.at[pl.ds(0, HEADS - 1)], chain_recv.at[5])

    out = jnp.zeros((16, 128), jnp.float32)
    for h in range(HEADS):
        out = out + jnp.dot(
            agb[h], wo[128 * h : 128 * h + 128, :], preferred_element_type=jnp.float32
        )
    osend[...] = out
    tbuf[mt] = out
    for dt in (4, 5, 3, 2, 6, 1, 7):
        remote(
            osend, tbuf.at[mt], chain_send.at[6], chain_recv.at[6], {"tp": (mt + dt) % TP}
        ).start()
    bulk(6)
    wait_bytes(tbuf.at[pl.ds(0, TP - 1)], chain_recv.at[6])
    out = jnp.sum(tbuf[...], axis=0)
    for step in range(3):
        for seq in range(4):
            r = 3 * seq + step
            fs[step, seq : seq + 1, :] = out[r : r + 1, :]
    att_ref[...] = fs[...].astype(jnp.bfloat16)

    wait_bytes(xbuf.at[pl.ds(0, XN - 1)], chain_send.at[0])
    wait_bytes(zbuf.at[pl.ds(0, ZN - 1)], chain_send.at[1])
    wait_bytes(zbuf.at[pl.ds(0, 15)], chain_send.at[2])
    wait_bytes(zb2.at[pl.ds(0, ZN - 1)], chain_send.at[3])
    wait_bytes(x2buf.at[pl.ds(0, XN - 1)], chain_send.at[4])
    wait_bytes(agb.at[pl.ds(0, HEADS - 1)], chain_send.at[5])
    wait_bytes(tbuf.at[pl.ds(0, TP - 1)], chain_send.at[6])
    cp_own.wait()
    others = pl.ds(0, 2 * (ZN * XN - 1))
    wait_bytes(packed.at[others], a2a_send)
    wait_bytes(rel_ref.at[others], a2a_recv)


NEAR = (((1, -1, 2, -2), 0, 4), ((0,), 1, 4))
PLAN = (NEAR, (((8,), 0, 4), ((7, -7), 0, 2)), (((7, -7), 2, 4),), (((6, -6), 0, 4), ((5, -5), 0, 4)), (), (((4, -4), 0, 4), ((3, -3), 0, 4)), ())


def inverse_table():
    half = np.arange(64, dtype=np.float32)
    power = np.float32(-math.log(500000.0)) * half * np.float32(2.0) / np.float32(128.0)
    inverse = np.exp(power.astype(np.float64)).astype(np.float32)
    return np.concatenate([inverse, inverse])[None, :]


def body(
    new_hidden, norm_gain, qkv_weight, out_weight, owned_cache, lengths, owner_device, block_target
):
    f32, bf16, i32 = jnp.float32, jnp.bfloat16, jnp.int32
    vmem = pl.BlockSpec(memory_space=pltpu.VMEM)
    smem = pl.BlockSpec(memory_space=pltpu.SMEM)
    hbm = pl.BlockSpec(memory_space=pltpu.HBM)
    dma = pltpu.SemaphoreType.DMA
    attended, relaid = pl.pallas_call(
        kernel,
        out_shape=(
            pltpu.VMEM((3, 4, 128), bf16),
            pltpu.VMEM((128, 16, 256), bf16),
        ),
        in_specs=[smem] + [hbm] * 8,
        out_specs=(vmem, vmem),
        scratch_shapes=[
            pltpu.VMEM((3, 4, 128), bf16),
            pltpu.VMEM((1, 128), f32),
            pltpu.VMEM((1, 128), f32),
            pltpu.VMEM((1, 64), i32),
            pltpu.VMEM((1, 128), i32),
            pltpu.VMEM((64, 128), i32),
            pltpu.SMEM((64, 128), i32),
            pltpu.VMEM((128, 1280), bf16),
            pltpu.VMEM((1024, 128), bf16),
            pltpu.VMEM((128, 16, 256), bf16),
            pltpu.VMEM((128, 16, 256), bf16),
            pltpu.VMEM((16, 128), f32),
            pltpu.VMEM((128, 128), f32),
            pltpu.VMEM((4, 32, 128), f32),
            pltpu.VMEM((4, 8, 128), f32),
            pltpu.VMEM((16, 8, 128), f32),
            pltpu.VMEM((8, 128), f32),
            pltpu.VMEM((4, 4, 8, 128), f32),
            pltpu.VMEM((32, 128), f32),
            pltpu.VMEM((8, 4, 128), f32),
            pltpu.VMEM((16, 4, 128), f32),
            pltpu.VMEM((32, 128), f32),
            pltpu.VMEM((4, 32, 128), f32),
            pltpu.VMEM((16, 128), bf16),
            pltpu.VMEM((8, 16, 128), bf16),
            pltpu.VMEM((16, 128), f32),
            pltpu.VMEM((8, 16, 128), f32),
            pltpu.VMEM((3, 4, 128), f32),
            dma((9,)),
            dma,
            dma,
            dma,
            dma((7,)),
            dma((7,)),
            pltpu.SemaphoreType.REGULAR,
        ],
        compiler_params=pltpu.CompilerParams(
            collective_id=0, has_side_effects=True, vmem_limit_bytes=VL * 1024 * 1024
        ),
        name="decode_and_relay",
    )(
        lengths,
        new_hidden,
        norm_gain.reshape(1, 128),
        jnp.asarray(inverse_table()),
        owner_device.reshape(1, 64),
        block_target.reshape(64, 1, 128),
        qkv_weight.reshape(128, 1280),
        out_weight.reshape(1024, 128),
        owned_cache.reshape(128, 16, 256),
    )
    return attended, relaid.reshape(128, 16, 1, 256)


def solution(mesh):
    in_specs = (
        P(None, None, "ctx"),
        P("ctx"),
        P("ctx", "tp", None),
        P("tp", None, "ctx"),
        P("ctx", None, "tp", None),
        P(),
        P(),
        P(),
    )
    out_specs = (P(None, None, "ctx"), P("ctx", None, "tp", None))
    return jax.shard_map(body, mesh=mesh, in_specs=in_specs, out_specs=out_specs, check_vma=False)
```
